32 devices in a mesh: dom: 8 (over z, y), rep: 4 (over x, core).
Axes of the slice: x: 2, y: 2, z: 4, core: 2. Of those that a mesh axis runs over, the one named last changes fastest.
Arguments:
- features: bfloat16 [12288, 256], P('dom'), may hold values from -6 to 6
- tile_weights: bfloat16 [8, 4, 2, 88, 128, 128], P('dom', 'rep'), may hold values from 0 to 0.023071289
- tile_rows: int32 [8, 4, 2, 88], P('dom', 'rep'), may hold values from 0 to 11, as said below
- tile_cols: int32 [8, 4, 2, 88], P('dom', 'rep'), may hold values from 0 to 11, as said below
- tile_counts: int32 [8, 4, 2], P('dom', 'rep'), may hold values from 1 to 88, as said below
- weight_self: bfloat16 [256, 256], replicated, may hold values from -0.375 to 0.375
- weight_neigh: bfloat16 [256, 256], replicated, may hold values from -0.375 to 0.375
- cotangent: bfloat16 [12288, 256], P(('dom', 'rep')), may hold values from -0.053955078 to 0.053955078
Outputs:
- out: bfloat16 [12288, 256], P(('dom', 'rep'))
- grad_self: float32 [256, 256], replicated
- grad_neigh: float32 [256, 256], replicated
The draws below stay inside these ranges and needn't reach their ends.
Inputs may be any that keep to these rules, and one draw needn't show every extreme that they name: For each p, r, s the first tile_counts[p, r, s] slots name distinct pairs (tile_rows, tile_cols); slots from tile_counts[p, r, s] on are unused. `tile_cols`: see tile_rows. `tile_counts`: some device fills all 88 slots of some column step.
All inputs are finite; a program needn't handle non-finite values.
Results may differ from the reference program's by a relative error of at most 0.0052.
Values may be sent and summed in bfloat16 or wider, within the bound.
No kernel may reach another device: no remote copies, remote signals or barrier semaphores. Data moves between devices by JAX's collectives and lax.ppermute only.
A program may use at most 128 MiB of HBM per device.

```python
import jax
import jax.numpy as jnp
from jax import lax

F = 256
TILE = 128
RT = 12
KS = 88
BLOCKS = 8
GROUPS = 4
STEPS = 2
NODES = 12288
N_DOM = 8
N_REP = 4


def tile_positions(key):
    base = jax.random.fold_in(key, 7)
    keys = jax.random.split(base, BLOCKS * GROUPS * STEPS)

    def permute_one(single_key):
        return jax.random.permutation(single_key, RT * RT)[:KS]
    chosen = jax.vmap(permute_one)(keys)
    return chosen.reshape(BLOCKS, GROUPS, STEPS, KS).astype(jnp.int32)


def draw_tile_rows(key, part):
    return tile_positions(key) // RT


def draw_tile_cols(key, part):
    return tile_positions(key) % RT


def draw_tile_counts(key, part):
    base = jax.random.fold_in(key, 3)
    first_key, second_key, third_key = jax.random.split(base, 3)
    divisor = jax.random.randint(first_key, (BLOCKS, GROUPS, 1), 1, 5)
    jitter = jax.random.randint(second_key, (BLOCKS, GROUPS, STEPS), 0, max(KS // 8, 1))
    counts = jnp.maximum(KS // divisor - jitter, 1).astype(jnp.int32)
    total = BLOCKS * GROUPS * STEPS
    chosen = jax.random.randint(third_key, (), 0, total)
    flat = jnp.where(jnp.arange(total) == chosen, KS, counts.reshape(total))
    return flat.reshape(BLOCKS, GROUPS, STEPS).astype(jnp.int32)


def block_levels(own_key, extent, pieces, smallest, top_value):
    loudness, own = 1.0, jax.random.fold_in(own_key, 6)
    for axis_at, parts in pieces:
        draws = jnp.exp(jax.random.uniform(jax.random.fold_in(own, axis_at), (parts,), jnp.float32, smallest / len(pieces), top_value / len(pieces)))
        loudness = loudness * jnp.repeat(draws, extent[axis_at] // parts).reshape([-1 if axis == axis_at else 1 for axis in range(len(extent))])
    return loudness


def bell_draw(own_key, shape, spread, limit, cuts=(), kind=jnp.bfloat16):
    entries = spread * jax.random.normal(own_key, shape, jnp.float32)
    if cuts:
        entries = entries * block_levels(own_key, shape, cuts, -0.22, 0.18)
    return jnp.clip(entries, -limit, limit).astype(kind)


def setup_inputs(seed: int = 0) -> dict:
    seeds = jax.random.split(jax.random.key(seed), 9)
    return {
        "features": bell_draw(seeds[0], (NODES, F), 1.0, 6.0, ((0, 8),)),
        "tile_weights": jnp.clip(0.023071289 * jax.random.uniform(seeds[1], (BLOCKS, GROUPS, STEPS, KS, TILE, TILE), jnp.float32) ** block_levels(seeds[1], (BLOCKS, GROUPS, STEPS, KS, TILE, TILE), ((0, 8), (1, 4)), -0.2, 0.2), 0.0, 0.023071289).astype(jnp.bfloat16),
        "tile_rows": draw_tile_rows(jax.random.fold_in(seeds[8], 71), 0),
        "tile_cols": draw_tile_cols(jax.random.fold_in(seeds[8], 71), 0),
        "tile_counts": draw_tile_counts(jax.random.fold_in(seeds[8], 71), 0),
        "weight_self": bell_draw(seeds[5], (F, F), F ** -0.5, 0.375),
        "weight_neigh": bell_draw(seeds[6], (F, F), F ** -0.5, 0.375),
        "cotangent": bell_draw(seeds[7], (NODES, F), (1.0 / NODES ** 0.5), 0.053955078, ((0, 32),)),
    }


def block_aggregate(features, tile_weights, tile_rows, tile_cols, tile_counts, block_index):
    tiled = features.reshape(N_DOM, RT, TILE, F)
    group_ids = jnp.arange(N_REP, dtype=jnp.int32)[:, None]
    step_ids = jnp.arange(STEPS, dtype=jnp.int32)[None, :]
    column_block = (block_index + group_ids * STEPS + step_ids - STEPS // 2 + N_DOM) % N_DOM
    cols_now = tile_cols[block_index]
    picked = tiled[column_block[:, :, None], cols_now].astype(jnp.float32)
    live_slots = (jnp.arange(KS, dtype=jnp.int32)[None, None, :] < tile_counts[block_index][:, :, None])
    weights_now = tile_weights[block_index].astype(jnp.float32) * live_slots.astype(jnp.float32)[:, :, :, None, None]
    product = jnp.einsum('gskij,gskjf->gskif', weights_now, picked)
    rows_now = tile_rows[block_index].reshape(N_REP * STEPS * KS)
    partial_value = jnp.zeros((RT, TILE, F), product.dtype)
    partial_value = partial_value.at[rows_now].add(product.reshape(N_REP * STEPS * KS, TILE, F))
    return partial_value


def reference(features, tile_weights, tile_rows, tile_cols, tile_counts, weight_self, weight_neigh, cotangent):
    def one_block(block_index):
        return block_aggregate(features, tile_weights, tile_rows, tile_cols, tile_counts, block_index)

    summed = lax.map(one_block, jnp.arange(N_DOM, dtype=jnp.int32))
    aggregate = summed.reshape(NODES, F).astype(jnp.bfloat16)
    pre = jnp.dot(features, weight_self, preferred_element_type=jnp.float32)
    pre = pre + jnp.dot(aggregate, weight_neigh, preferred_element_type=jnp.float32)
    output = jax.nn.silu(pre).astype(jnp.bfloat16)
    sigmoid = jax.nn.sigmoid(pre)
    slope = (cotangent.astype(jnp.float32) * sigmoid * (1.0 + pre * (1.0 - sigmoid))).astype(jnp.bfloat16)
    grad_self = jnp.dot(features.T, slope, preferred_element_type=jnp.float32)
    grad_neigh = jnp.dot(aggregate.T, slope, preferred_element_type=jnp.float32)
    return (output, grad_self, grad_neigh)
```

```python
import functools

import jax
import jax.numpy as jnp
from jax import lax
from jax.experimental import pallas as pl
from jax.experimental.pallas import tpu as pltpu
from jax.sharding import PartitionSpec as P

AXES = ("dom", "rep")
F32, BF16 = jnp.float32, jnp.bfloat16
MIB = 1 << 20


def flat_permute(value, blocks, groups, source):
    route = []
    for p in range(blocks):
        for r in range(groups):
            q, g = source(p, r)
            route.append((q % blocks * groups + g % groups, p * groups + r))
    return lax.ppermute(value, AXES, route)


def rep_exchange(value, groups, bit):
    route = [(r, r ^ (1 << bit)) for r in range(groups)]
    return lax.ppermute(value, "rep", route)


def fetch_blocks(features, blocks, groups, steps):
    found = []
    for s in range(steps):
        flip = groups // 2 if s % 2 else 0

        def source(p, r, s=s, flip=flip):
            return p + r * steps + s - steps // 2, r ^ flip

        found.append(flat_permute(features, blocks, groups, source))
    return found


def densify_kernel(counts, rows, cols, weights, dense, zero_rows, sem):
    steps, _, tile, _ = weights.shape
    row_tiles = dense.shape[1] // tile
    zero_rows[...] = jnp.zeros_like(zero_rows)

    def clear(i):
        s, row = i // row_tiles, i % row_tiles
        return pltpu.make_async_copy(zero_rows, dense.at[s, pl.ds(row * tile, tile), :], sem)

    def place(s, k):
        row = pl.multiple_of(rows[s, k] * tile, tile)
        col = pl.multiple_of(cols[s, k] * tile, tile)
        return pltpu.make_async_copy(
            weights.at[s, k], dense.at[s, pl.ds(row, tile), pl.ds(col, tile)], sem
        )

    @pl.loop(0, steps * row_tiles)
    def _(i):
        clear(i).start()

    @pl.loop(0, steps * row_tiles)
    def _(i):
        clear(i).wait()

    for s in range(steps):

        @pl.loop(0, counts[s])
        def _(k, s=s):
            place(s, k).start()

    for s in range(steps):

        @pl.loop(0, counts[s])
        def _(k, s=s):
            place(s, k).wait()


def densify(weights, rows, cols, counts, nodes):
    steps, _, tile, _ = weights.shape
    smem = pl.BlockSpec(memory_space=pltpu.SMEM)
    hbm = pl.BlockSpec(memory_space=pl.ANY)
    return pl.pallas_call(
        densify_kernel,
        out_shape=jax.ShapeDtypeStruct((steps, nodes, nodes), BF16),
        in_specs=[smem, smem, smem, hbm],
        out_specs=hbm,
        scratch_shapes=[pltpu.VMEM((tile, nodes), BF16), pltpu.SemaphoreType.DMA],
        compiler_params=pltpu.CompilerParams(vmem_limit_bytes=4 * MIB),
        cost_estimate=pl.CostEstimate(
            flops=0, bytes_accessed=2 * weights.size * 2 + steps * nodes * nodes * 2, transcendentals=0
        ),
        name="densify",
    )(counts, rows, cols, weights)


def aggregate_kernel(half, order, dense, *refs):
    blocks, (send, keep) = refs[:-2], refs[-2:]
    i = pl.program_id(0)
    total = jnp.dot(dense[0], blocks[0][...], preferred_element_type=F32)
    for s in range(1, len(blocks)):
        total = total + jnp.dot(dense[s], blocks[s][...], preferred_element_type=F32)

    @pl.when(i < half)
    def _():
        send[0] = total

    @pl.when(i >= half)
    def _():
        keep[0] = total


def aggregate_parts(dense, blocks, groups, core):
    steps, nodes, _ = dense.shape
    width = blocks[0].shape[1]
    part, half = nodes // groups, groups // 2
    halves = jnp.arange(half, dtype=jnp.int32) * 2
    order = jnp.concatenate([halves + 1 - core, halves + core])
    whole = pl.BlockSpec((nodes, width), lambda i, order: (0, 0))
    shape = jax.ShapeDtypeStruct((half, part, width), F32)
    return pl.pallas_call(
        functools.partial(aggregate_kernel, half),
        out_shape=(shape, shape),
        grid_spec=pltpu.PrefetchScalarGridSpec(
            num_scalar_prefetch=1,
            grid=(groups,),
            in_specs=[pl.BlockSpec((steps, part, nodes), lambda i, order: (0, order[i], 0))]
            + [whole] * steps,
            out_specs=(
                pl.BlockSpec((1, part, width), lambda i, order: (jnp.minimum(i, half - 1), 0, 0)),
                pl.BlockSpec((1, part, width), lambda i, order: (jnp.maximum(i - half, 0), 0, 0)),
            ),
        ),
        compiler_params=pltpu.CompilerParams(vmem_limit_bytes=44 * MIB),
        cost_estimate=pl.CostEstimate(
            flops=2 * steps * nodes * nodes * width,
            bytes_accessed=dense.size * 2 + steps * nodes * width * 2 + nodes * width * 4,
            transcendentals=0,
        ),
        name="aggregate_parts",
    )(order, dense, *blocks)


def layer_kernel(
    place, features, kept, received, side, weight_self, weight_neigh, cotangent, out, grad_keep, grad_send
):
    own = features[...]
    summed = kept[0] + received[0] + side[...].astype(F32)
    aggregate = summed.astype(BF16)
    pre = jnp.dot(own, weight_self[...], preferred_element_type=F32)
    pre = pre + jnp.dot(aggregate, weight_neigh[...], preferred_element_type=F32)
    sigmoid = jax.nn.sigmoid(pre)
    out[...] = (pre * sigmoid).astype(BF16)
    slope = (cotangent[...].astype(F32) * sigmoid * (1.0 + pre * (1.0 - sigmoid))).astype(BF16)
    contract = (((0,), (0,)), ((), ()))
    grad_self = lax.dot_general(own, slope, contract, preferred_element_type=F32)
    grad_neigh = lax.dot_general(aggregate, slope, contract, preferred_element_type=F32)
    rows, lanes = grad_self.shape[0], grad_keep.shape[1]
    first = place[2] == 0
    for at in range(grad_self.shape[1] // lanes):
        a, b = (g[:, at * lanes : (at + 1) * lanes] for g in (grad_self, grad_neigh))
        grad_keep[at * rows : (at + 1) * rows, :] = jnp.where(first, a, b)
        grad_send[at * rows : (at + 1) * rows, :] = jnp.where(first, b, a)


def layer(place, features, kept, received, side, weight_self, weight_neigh, cotangent):
    part, width = side.shape
    lanes = width // 2
    square = pl.BlockSpec((width, width), lambda i, place: (0, 0))
    rows = pl.BlockSpec((part, width), lambda i, place: (0, 0))
    third = pl.BlockSpec((1, part, width), lambda i, place: (place[1], 0, 0))
    grads = pl.BlockSpec((width * width // lanes, lanes), lambda i, place: (0, 0))
    grad_shape = jax.ShapeDtypeStruct((width * width // lanes, lanes), F32)
    return pl.pallas_call(
        layer_kernel,
        out_shape=(jax.ShapeDtypeStruct((part, width), BF16), grad_shape, grad_shape),
        grid_spec=pltpu.PrefetchScalarGridSpec(
            num_scalar_prefetch=1,
            grid=(1,),
            in_specs=[
                pl.BlockSpec((part, width), lambda i, place: (place[0], 0)),
                third,
                third,
                rows,
                square,
                square,
                rows,
            ],
            out_specs=(rows, grads, grads),
        ),
        compiler_params=pltpu.CompilerParams(vmem_limit_bytes=16 * MIB),
        name="layer",
    )(place, features, kept, received, side, weight_self, weight_neigh, cotangent)


def unpack_kernel(place, mine, other, grad_self, grad_neigh):
    rows, lanes = grad_self.shape[0], mine.shape[1]
    first = place[2] == 0
    for at in range(grad_self.shape[1] // lanes):
        a = mine[at * rows : (at + 1) * rows, :].astype(F32)
        b = other[at * rows : (at + 1) * rows, :].astype(F32)
        grad_self[:, at * lanes : (at + 1) * lanes] = jnp.where(first, a, b)
        grad_neigh[:, at * lanes : (at + 1) * lanes] = jnp.where(first, b, a)


def unpack(place, mine, other, width):
    shape = jax.ShapeDtypeStruct((width, width), F32)
    vmem = pl.BlockSpec(memory_space=pltpu.VMEM)
    return pl.pallas_call(
        unpack_kernel,
        out_shape=(shape, shape),
        in_specs=[pl.BlockSpec(memory_space=pltpu.SMEM), vmem, vmem],
        out_specs=(vmem, vmem),
        name="unpack",
    )(place, mine, other)


def all_reduce_grads(place, keep, send, devices, groups, width):
    packed, lanes = keep.shape
    chunk = packed // devices
    chip = (keep + rep_exchange(send, groups, 0)).astype(BF16)
    terms = lax.all_to_all(chip, AXES, 0, 0, tiled=True)
    summed = terms.reshape(devices // 2, 2, chunk, lanes).astype(F32).sum(0).astype(BF16)
    spread = jnp.broadcast_to(summed[None], (devices // 2, 2, chunk, lanes)).reshape(packed, lanes)
    mine = lax.all_to_all(spread, AXES, 0, 0, tiled=True)
    other = rep_exchange(mine, groups, 0)
    return unpack(place, mine, other, width)


def on_device(
    features, tile_weights, tile_rows, tile_cols, tile_counts, weight_self, weight_neigh, cotangent
):
    blocks, groups = lax.axis_size("dom"), lax.axis_size("rep")
    steps = tile_weights.shape[2]
    nodes, width = features.shape
    rep = lax.axis_index("rep").astype(jnp.int32)
    core, side_at = rep % 2, rep // 2
    place = jnp.stack([rep, side_at, core])

    found = fetch_blocks(features, blocks, groups, steps)
    dense = densify(tile_weights[0, 0], tile_rows[0, 0], tile_cols[0, 0], tile_counts[0, 0], nodes)
    send, kept = aggregate_parts(dense, found, groups, core)
    received = rep_exchange(send, groups, 0)
    across = lax.dynamic_index_in_dim(kept, 1 - side_at, 0, keepdims=False)
    across = across + lax.dynamic_index_in_dim(received, 1 - side_at, 0, keepdims=False)
    side = rep_exchange(across.astype(BF16), groups, 1)
    out, grad_keep, grad_send = layer(
        place, features, kept, received, side, weight_self, weight_neigh, cotangent
    )
    grad_self, grad_neigh = all_reduce_grads(
        place, grad_keep, grad_send, blocks * groups, groups, width
    )
    return out, grad_self, grad_neigh


def solution(mesh):
    return jax.shard_map(
        on_device,
        mesh=mesh,
        in_specs=(
            P("dom", None),
            P("dom", "rep", None, None, None, None),
            P("dom", "rep", None, None),
            P("dom", "rep", None, None),
            P("dom", "rep", None),
            P(),
            P(),
            P(AXES, None),
        ),
        out_specs=(P(AXES, None), P(), P()),
        check_vma=False,
    )
```

```python
import functools

import jax
import jax.numpy as jnp
from jax import lax
from jax.experimental import pallas as pl
from jax.experimental.pallas import tpu as pltpu
from jax.sharding import PartitionSpec as P

AXES = ("dom", "rep")
F32, BF16 = jnp.float32, jnp.bfloat16
MIB = 1 << 20


def flat_permute(value, blocks, groups, source):
    route = []
    for p in range(blocks):
        for r in range(groups):
            q, g = source(p, r)
            route.append((q % blocks * groups + g % groups, p * groups + r))
    return lax.ppermute(value, AXES, route)


def rep_exchange(value, groups, bit):
    route = [(r, r ^ (1 << bit)) for r in range(groups)]
    return lax.ppermute(value, "rep", route)


def fetch_blocks(features, blocks, groups, steps):
    found = []
    for s in range(steps):
        flip = groups // 2 if s % 2 else 0

        def source(p, r, s=s, flip=flip):
            return p + r * steps + s - steps // 2, r ^ flip

        found.append(flat_permute(features, blocks, groups, source))
    return found


def densify_kernel(place, counts, rows, cols, weights, send, mid, own, zero_rows, sem):
    steps, _, tile, _ = weights.shape
    nodes = zero_rows.shape[1]
    per_part = own.shape[1] // tile
    zero_rows[...] = jnp.zeros_like(zero_rows)

    def clear(ref, i):
        per_step = ref.shape[1] // tile
        s, row = i // per_step, i % per_step
        return pltpu.make_async_copy(zero_rows, ref.at[s, pl.ds(row * tile, tile), :], sem)

    def put(ref, s, k, row):
        row = pl.multiple_of(row * tile, tile)
        col = pl.multiple_of(cols[s, k] * tile, tile)
        return pltpu.make_async_copy(
            weights.at[s, k], ref.at[s, pl.ds(row, tile), pl.ds(col, tile)], sem
        )

    for ref in (send, mid, own):

        @pl.loop(0, steps * (ref.shape[1] // tile))
        def _(i, ref=ref):
            clear(ref, i).start()

    for ref in (send, mid, own):

        @pl.loop(0, steps * (ref.shape[1] // tile))
        def _(i, ref=ref):
            clear(ref, i).wait()

    for s in range(steps):

        @pl.loop(0, counts[s])
        def _(k, s=s):
            part, row = rows[s, k] // per_part, rows[s, k] % per_part
            sent = part % 2 != place[2]
            kept = jnp.logical_and(jnp.logical_not(sent), part // 2 == place[1])

            @pl.when(sent)
            def _():
                put(send, s, k, part // 2 * per_part + row).start()

            @pl.when(kept)
            def _():
                put(own, s, k, row).start()

            @pl.when(jnp.logical_not(jnp.logical_or(sent, kept)))
            def _():
                put(mid, s, k, row).start()

    for s in range(steps):

        @pl.loop(0, counts[s])
        def _(k, s=s):
            put(own, s, 0, 0).wait()


def densify(place, weights, rows, cols, counts, nodes, groups):
    steps, _, tile, _ = weights.shape
    part = nodes // groups
    smem = pl.BlockSpec(memory_space=pltpu.SMEM)
    hbm = pl.BlockSpec(memory_space=pl.ANY)
    return pl.pallas_call(
        densify_kernel,
        out_shape=tuple(
            jax.ShapeDtypeStruct((steps, n * part, nodes), BF16) for n in (groups // 2, 1, 1)
        ),
        in_specs=[smem, smem, smem, smem, hbm],
        out_specs=(hbm, hbm, hbm),
        scratch_shapes=[pltpu.VMEM((tile, nodes), BF16), pltpu.SemaphoreType.DMA],
        compiler_params=pltpu.CompilerParams(vmem_limit_bytes=4 * MIB),
        cost_estimate=pl.CostEstimate(
            flops=0, bytes_accessed=2 * weights.size * 2 + steps * nodes * nodes * 2, transcendentals=0
        ),
        name="densify",
    )(place, counts, rows, cols, weights)


def block_product(dense, found):
    total = jnp.dot(dense[0], found[0][...], preferred_element_type=F32)
    for s in range(1, len(found)):
        total = total + jnp.dot(dense[s], found[s][...], preferred_element_type=F32)
    return total


def rows_kernel(found_total, place, dense, *refs):
    refs[-1][...] = block_product(dense, refs[:found_total])


def own_kernel(place, features, received, weight_self, dense, *refs):
    found, (own, projected) = refs[:-2], refs[-2:]
    part = own.shape[0]
    own[...] = block_product(dense, found) + received[pl.ds(pl.multiple_of(place[1] * part, part), part), :]
    mine = features[pl.ds(pl.multiple_of(place[0] * part, part), part), :]
    projected[...] = jnp.dot(mine, weight_self[...], preferred_element_type=F32)


def product_call(kernel, place, out_shape, others, dense, found, name):
    vmem = pl.BlockSpec(memory_space=pltpu.VMEM)
    operands = (*others, dense, *found)
    outs = jax.tree.leaves(out_shape)
    held = sum(v.size * v.dtype.itemsize for v in (*operands, *outs))
    width = found[0].shape[1]
    rows = sum(v.size // width for v in outs[:1])
    return pl.pallas_call(
        kernel,
        out_shape=out_shape,
        in_specs=[pl.BlockSpec(memory_space=pltpu.SMEM)] + [vmem] * len(operands),
        out_specs=jax.tree.map(lambda _: vmem, out_shape),
        compiler_params=pltpu.CompilerParams(vmem_limit_bytes=held + 8 * MIB),
        cost_estimate=pl.CostEstimate(
            flops=2 * rows * dense.shape[0] * dense.shape[1] * width,
            bytes_accessed=rows * dense.shape[0] * dense.shape[1] * 2,
            transcendentals=0,
        ),
        name=name,
    )(place, *operands)


def layer_kernel(
    place, features, own, side, projected, weight_neigh, cotangent, out, grad_keep, grad_send
):
    part = own.shape[0]
    mine = features[pl.ds(pl.multiple_of(place[0] * part, part), part), :]
    aggregate = (own[...] + side[...].astype(F32)).astype(BF16)
    pre = projected[...] + jnp.dot(aggregate, weight_neigh[...], preferred_element_type=F32)
    sigmoid = jax.nn.sigmoid(pre)
    out[...] = (pre * sigmoid).astype(BF16)
    slope = (cotangent[...].astype(F32) * sigmoid * (1.0 + pre * (1.0 - sigmoid))).astype(BF16)
    contract = (((0,), (0,)), ((), ()))
    grad_self = lax.dot_general(mine, slope, contract, preferred_element_type=F32)
    grad_neigh = lax.dot_general(aggregate, slope, contract, preferred_element_type=F32)
    first = place[2] == 0
    grad_keep[...] = jnp.where(first, grad_self, grad_neigh)
    grad_send[...] = jnp.where(first, grad_neigh, grad_self)


def layer(place, features, own, side, projected, weight_neigh, cotangent):
    part, width = side.shape
    vmem = pl.BlockSpec(memory_space=pltpu.VMEM)
    grad = jax.ShapeDtypeStruct((width, width), F32)
    return pl.pallas_call(
        layer_kernel,
        out_shape=(jax.ShapeDtypeStruct((part, width), BF16), grad, grad),
        in_specs=[pl.BlockSpec(memory_space=pltpu.SMEM)] + [vmem] * 6,
        out_specs=(vmem, vmem, vmem),
        compiler_params=pltpu.CompilerParams(vmem_limit_bytes=16 * MIB),
        name="layer",
    )(place, features, own, side, projected, weight_neigh, cotangent)


def all_reduce_grads(core, keep, send, devices, groups):
    rows, width = keep.shape
    chunk = rows // devices
    chip = (keep + rep_exchange(send, groups, 0)).astype(BF16)
    terms = lax.all_to_all(chip, AXES, 0, 0, tiled=True)
    summed = terms.reshape(devices // 2, 2, chunk, width).astype(F32).sum(0).astype(BF16)
    spread = jnp.broadcast_to(summed[None], (devices // 2, 2, chunk, width)).reshape(rows, width)
    mine = lax.all_to_all(spread, AXES, 0, 0, tiled=True)
    other = rep_exchange(mine, groups, 0)
    first = core == 0
    grad_self = jnp.where(first, mine, other).astype(F32)
    grad_neigh = jnp.where(first, other, mine).astype(F32)
    return grad_self, grad_neigh


def on_device(
    features, tile_weights, tile_rows, tile_cols, tile_counts, weight_self, weight_neigh, cotangent
):
    blocks, groups = lax.axis_size("dom"), lax.axis_size("rep")
    steps = tile_weights.shape[2]
    nodes, width = features.shape
    rep = lax.axis_index("rep").astype(jnp.int32)
    core, side_at = rep % 2, rep // 2
    place = jnp.stack([rep, side_at, core])

    found = fetch_blocks(features, blocks, groups, steps)
    dense_send, dense_mid, dense_own = densify(
        place, tile_weights[0, 0], tile_rows[0, 0], tile_cols[0, 0], tile_counts[0, 0], nodes, groups
    )
    part = nodes // groups
    rows = functools.partial(rows_kernel, steps)
    quarter = jax.ShapeDtypeStruct((part, width), F32)
    halves = jax.ShapeDtypeStruct((nodes // 2, width), F32)
    send = product_call(
        rows, place, halves, (), dense_send, found, "send_rows"
    )
    received = rep_exchange(send, groups, 0)
    mid = product_call(
        rows, place, quarter, (), dense_mid, found, "mid_rows"
    )
    across = mid + lax.dynamic_slice_in_dim(received, (1 - side_at) * part, part, 0)
    side = rep_exchange(across.astype(BF16), groups, 1)
    own, projected = product_call(
        own_kernel, place, (quarter, quarter), (features, received, weight_self), dense_own, found, "own_rows"
    )
    out, grad_keep, grad_send = layer(
        place, features, own, side, projected, weight_neigh, cotangent
    )
    grad_self, grad_neigh = all_reduce_grads(core, grad_keep, grad_send, blocks * groups, groups)
    return out, grad_self, grad_neigh


def solution(mesh):
    return jax.shard_map(
        on_device,
        mesh=mesh,
        in_specs=(
            P("dom", None),
            P("dom", "rep", None, None, None, None),
            P("dom", "rep", None, None),
            P("dom", "rep", None, None),
            P("dom", "rep", None),
            P(),
            P(),
            P(AXES, None),
        ),
        out_specs=(P(AXES, None), P(), P()),
        check_vma=False,
    )
```

```python
import functools

import jax
import jax.numpy as jnp
from jax import lax
from jax.experimental import pallas as pl
from jax.experimental.pallas import tpu as pltpu
from jax.sharding import PartitionSpec as P

AXES = ("dom", "rep")
F32, BF16 = jnp.float32, jnp.bfloat16
MIB = 1 << 20
SHIFT = 16


def position():
    rep = lax.axis_index("rep").astype(jnp.int32)
    return rep, rep // 2, rep % 2


def flat_permute(value, blocks, groups, source):
    route = []
    for p in range(blocks):
        for r in range(groups):
            at = source(p, r)
            if at is not None:
                route.append((at[0] % blocks * groups + at[1] % groups, p * groups + r))
    return lax.ppermute(value, AXES, route)


def rep_exchange(value, groups, bit):
    route = [(r, r ^ (1 << bit)) for r in range(groups)]
    return lax.ppermute(value, "rep", route)


def fetch_blocks(features, blocks, groups, steps):
    found = []
    for s in range(steps):
        flip = groups // 2 if s % 2 else 0

        def source(p, r, s=s, flip=flip):
            ahead = r * steps + s - steps // 2
            return (p + ahead, r ^ flip) if ahead or steps > 2 else None

        found.append(flat_permute(features, blocks, groups, source))
    return found


def densify_kernel(pieces, table, weights, *refs):
    outs, (zero_rows, sem) = refs[:-2], refs[-2:]
    tile = weights.shape[2]
    slots = weights.shape[1]
    filled = [
        (outs[at].at[i] if len(outs[at].shape) == 3 else outs[at], s, first)
        for at, i, s, first in pieces
    ]
    zero_rows[...] = jnp.zeros_like(zero_rows)

    def clear(ref, i):
        return pltpu.make_async_copy(zero_rows, ref.at[pl.ds(i * tile, tile), :], sem)

    for ref, _, _ in filled:

        @pl.loop(0, ref.shape[0] // tile)
        def _(i, ref=ref):
            clear(ref, i).start()

    for ref, _, _ in filled:

        @pl.loop(0, ref.shape[0] // tile)
        def _(i, ref=ref):
            clear(ref, i).wait()

    started = jnp.int32(0)
    for ref, s, first in filled:
        held = ref.shape[0] // tile
        whole = held * tile == zero_rows.shape[1]

        def place_slot(k, total, ref=ref, s=s, first=first, held=held, whole=whole):
            spot = table[s, k]
            row, col = (spot >> SHIFT) - first, spot & ((1 << SHIFT) - 1)

            def start():
                pltpu.make_async_copy(
                    weights.at[s, k],
                    ref.at[
                        pl.ds(pl.multiple_of(row * tile, tile), tile),
                        pl.ds(pl.multiple_of(col * tile, tile), tile),
                    ],
                    sem,
                ).start()

            if whole:
                start()
                return total + 1
            inside = jnp.logical_and(row >= 0, row < held)
            pl.when(inside)(start)
            return total + inside.astype(jnp.int32)

        started = lax.fori_loop(0, table[s, slots], place_slot, started)

    largest = 1
    while largest * 2 <= slots:
        largest *= 2

    def wait(tiles):
        some = weights.at[0, pl.ds(0, tiles)]
        pltpu.make_async_copy(some, some, sem).wait()

    @pl.loop(0, started // largest)
    def _(_):
        wait(largest)

    amount = largest // 2
    while amount:

        @pl.when(started & amount != 0)
        def _(amount=amount):
            wait(amount)

        amount //= 2


def densify(limit, table, weights, pieces, out_shape, name):
    tile = weights.shape[2]
    nodes = out_shape[0].shape[-1]
    hbm = pl.BlockSpec(memory_space=pl.ANY)
    size = sum(v.size for v in out_shape)
    return pl.pallas_call(
        functools.partial(densify_kernel, pieces),
        out_shape=out_shape,
        in_specs=[pl.BlockSpec(memory_space=pltpu.SMEM), hbm],
        out_specs=(hbm,) * len(out_shape),
        scratch_shapes=[pltpu.VMEM((tile, nodes), BF16), pltpu.SemaphoreType.DMA],
        compiler_params=pltpu.CompilerParams(vmem_limit_bytes=limit),
        cost_estimate=pl.CostEstimate(flops=0, bytes_accessed=6 * size, transcendentals=0),
        name=name,
    )(table, weights)


def spot_table(rows, cols, counts, order, part_tiles):
    part = rows // part_tiles
    row = rows % part_tiles
    for g, at in enumerate(order):
        row = row + jnp.where(part == g, at * part_tiles, 0)
    return jnp.concatenate([(row << SHIFT) + cols, counts[:, None]], axis=1)


def early_kernel(features, dense, *refs):
    found, outs = refs[:-3], refs[-3:]

    def run(blocks):
        at = 0
        for out in outs:
            rows = slice(at, at + out.shape[0])
            total = jnp.dot(dense[0, rows, :], blocks[0][...], preferred_element_type=F32)
            for s in range(1, len(blocks)):
                total = total + jnp.dot(dense[s, rows, :], blocks[s][...], preferred_element_type=F32)
            out[...] = total
            at += out.shape[0]

    if len(found) > 1:
        run(found)
        return
    rep, _, _ = position()
    pl.when(rep == 0)(lambda: run([features]))
    pl.when(rep != 0)(lambda: run(found))


def rows_kernel(begun, dense, block, out):
    out[...] = begun[...] + jnp.dot(dense[...], block[...], preferred_element_type=F32)


def mid_kernel(begun, dense, block, received, out):
    part = out.shape[0]
    _, side_at, _ = position()
    total = begun[...] + jnp.dot(dense[...], block[...], preferred_element_type=F32)
    total = total + received[pl.ds(pl.multiple_of((1 - side_at) * part, part), part), :]
    out[...] = total.astype(out.dtype)


def own_kernel(features, received, weight_self, begun, dense, block, own, projected):
    part = own.shape[0]
    rep, side_at, _ = position()
    own[...] = (
        begun[...]
        + jnp.dot(dense[...], block[...], preferred_element_type=F32)
        + received[pl.ds(pl.multiple_of(side_at * part, part), part), :]
    )
    mine = features[pl.ds(pl.multiple_of(rep * part, part), part), :]
    projected[...] = jnp.dot(mine, weight_self[...], preferred_element_type=F32)


def vmem_call(limit, kernel, out_shape, operands, name, flops=0):
    vmem = pl.BlockSpec(memory_space=pltpu.VMEM)
    held = sum(v.size * v.dtype.itemsize for v in (*operands, *jax.tree.leaves(out_shape)))
    return pl.pallas_call(
        kernel,
        out_shape=out_shape,
        in_specs=[vmem] * len(operands),
        out_specs=jax.tree.map(lambda _: vmem, out_shape),
        compiler_params=pltpu.CompilerParams(vmem_limit_bytes=limit),
        cost_estimate=pl.CostEstimate(flops=flops, bytes_accessed=held, transcendentals=0),
        name=name,
    )(*operands)


def layer_kernel(
    features, own, side, projected, weight_neigh, cotangent, out, grad_keep, grad_send
):
    part = own.shape[0]
    rep, _, core = position()
    mine = features[pl.ds(pl.multiple_of(rep * part, part), part), :]
    aggregate = (own[...] + side[...].astype(F32)).astype(BF16)
    pre = projected[...] + jnp.dot(aggregate, weight_neigh[...], preferred_element_type=F32)
    sigmoid = jax.nn.sigmoid(pre)
    out[...] = (pre * sigmoid).astype(BF16)
    slope = (cotangent[...].astype(F32) * sigmoid * (1.0 + pre * (1.0 - sigmoid))).astype(BF16)
    contract = (((0,), (0,)), ((), ()))
    grad_self = lax.dot_general(mine, slope, contract, preferred_element_type=F32)
    grad_neigh = lax.dot_general(aggregate, slope, contract, preferred_element_type=F32)
    first = core == 0
    grad_keep[...] = jnp.where(first, grad_self, grad_neigh)
    grad_send[...] = jnp.where(first, grad_neigh, grad_self)


def all_reduce_grads(core, keep, send, devices, groups):
    rows, width = keep.shape
    chunk = rows // devices
    chip = (keep + rep_exchange(send, groups, 0)).astype(BF16)
    terms = lax.all_to_all(chip, AXES, 0, 0, tiled=True)
    summed = terms.reshape(devices // 2, 2, chunk, width).astype(F32).sum(0).astype(BF16)
    spread = jnp.broadcast_to(summed[None], (devices // 2, 2, chunk, width)).reshape(rows, width)
    mine = lax.all_to_all(spread, AXES, 0, 0, tiled=True)
    other = rep_exchange(mine, groups, 0)
    first = core == 0
    grad_self = jnp.where(first, mine, other).astype(F32)
    grad_neigh = jnp.where(first, other, mine).astype(F32)
    return grad_self, grad_neigh


def on_device(
    features, tile_weights, tile_rows, tile_cols, tile_counts, weight_self, weight_neigh, cotangent
):
    blocks, groups = lax.axis_size("dom"), lax.axis_size("rep")
    steps = tile_weights.shape[2]
    nodes, width = features.shape
    rep, side_at, core = position()
    half = groups // 2
    others = [half + (jnp.int32(g // 2) == side_at) for g in range(groups)]
    order = [jnp.where(core == g % 2, others[g], g // 2) for g in range(groups)]
    part = nodes // groups
    part_tiles = part // tile_weights.shape[-1]
    table = spot_table(tile_rows[0, 0], tile_cols[0, 0], tile_counts[0, 0], order, part_tiles)
    weights = tile_weights[0, 0]
    limit = 2 * ((steps - 1) * nodes + (steps + 1) * width) * nodes + 4 * nodes * width + 8 * MIB
    row_parts = lambda n: jax.ShapeDtypeStruct((n * part, nodes), BF16)
    later = jax.ShapeDtypeStruct((steps - 1, nodes, nodes), BF16)
    send_piece = ((0, 0, 0, 0),)
    rest_pieces = tuple((0, s - 1, s, 0) for s in range(1, steps)) + (
        (1, 0, 0, half * part_tiles),
        (2, 0, 0, (half + 1) * part_tiles),
    )

    late_found, *early_found = fetch_blocks(features, blocks, groups, steps)
    (dense_send,) = densify(limit, table, weights, send_piece, (row_parts(half),), "densify_send")
    early, dense_mid, dense_own = densify(
        limit, table, weights, rest_pieces, (later, row_parts(1), row_parts(1)), "densify_rest"
    )
    quarter = jax.ShapeDtypeStruct((part, width), F32)
    halves = jax.ShapeDtypeStruct((nodes // 2, width), F32)
    square = jax.ShapeDtypeStruct((width, width), F32)
    per_row = 2 * nodes * width
    begun_send, begun_mid, begun_own = vmem_call(
        limit,
        early_kernel,
        (halves, quarter, quarter),
        (features, early, *early_found),
        "early_rows",
        (steps - 1) * nodes * per_row,
    )
    send = vmem_call(
        limit, rows_kernel, halves, (begun_send, dense_send, late_found), "send_rows", nodes // 2 * per_row
    )
    received = rep_exchange(send, groups, 0)
    across = vmem_call(
        limit,
        mid_kernel,
        jax.ShapeDtypeStruct((part, width), BF16),
        (begun_mid, dense_mid, late_found, received),
        "mid_rows",
        part * per_row,
    )
    side = rep_exchange(across, groups, 1)
    own, projected = vmem_call(
        limit,
        own_kernel,
        (quarter, quarter),
        (features, received, weight_self, begun_own, dense_own, late_found),
        "own_rows",
        part * per_row,
    )
    out, grad_keep, grad_send = vmem_call(
        limit,
        layer_kernel,
        (jax.ShapeDtypeStruct((part, width), BF16), square, square),
        (features, own, side, projected, weight_neigh, cotangent),
        "layer",
        6 * part * width * width,
    )
    grad_self, grad_neigh = all_reduce_grads(core, grad_keep, grad_send, blocks * groups, groups)
    return out, grad_self, grad_neigh


def solution(mesh):
    return jax.shard_map(
        on_device,
        mesh=mesh,
        in_specs=(
            P("dom", None),
            P("dom", "rep", None, None, None, None),
            P("dom", "rep", None, None),
            P("dom", "rep", None, None),
            P("dom", "rep", None),
            P(),
            P(),
            P(AXES, None),
        ),
        out_specs=(P(AXES, None), P(), P()),
        check_vma=False,
    )
```

```python
import functools

import jax
import jax.numpy as jnp
from jax import lax
from jax.experimental import pallas as pl
from jax.experimental.pallas import tpu as pltpu
from jax.sharding import PartitionSpec as P

AXES = ("dom", "rep")
F32, BF16 = jnp.float32, jnp.bfloat16
MIB = 1 << 20
SHIFT = 16


def position():
    rep = lax.axis_index("rep").astype(jnp.int32)
    return rep, rep // 2, rep % 2


def flat_permute(value, blocks, groups, source):
    route = []
    for p in range(blocks):
        for r in range(groups):
            at = source(p, r)
            if at is not None:
                route.append((at[0] % blocks * groups + at[1] % groups, p * groups + r))
    return lax.ppermute(value, AXES, route)


def rep_exchange(value, groups, bit):
    route = [(r, r ^ (1 << bit)) for r in range(groups)]
    return lax.ppermute(value, "rep", route)


def fetch_blocks(features, blocks, groups, steps):
    found = []
    for s in range(steps):
        flip = groups // 2 if s % 2 else 0

        def source(p, r, s=s, flip=flip):
            return p + r * steps + s - steps // 2, r ^ flip

        found.append(flat_permute(features, blocks, groups, source))
    return found


class Routes:
    def __init__(self, blocks, groups):
        self.blocks, self.half, self.last = blocks, groups // 2, groups - 1

    def ahead(self, p, r):
        if r == self.half:
            q = (p + 2 * r) % self.blocks
            return q, self.half if q // 2 % 2 else 0
        return (p + 2 * r - 1, 1) if r == 1 - p % 2 else None

    def passed(self, p, r):
        if p % 2 and r == self.half:
            return p - 1, r
        if p % 2 == 0 and r == self.last:
            return p + 1, r - 1
        return None

    def later(self, p, r):
        return (p + 2 * r, self.last + 1 - r) if r not in (0, self.half) else None

    def first(self, p, r):
        if self.passed(p, r) or r == 1 - p % 2:
            return None
        return p + 2 * r - 1, self.half if r in (0, self.last) else 1


def densify_kernel(pieces, table, weights, *refs):
    outs, (zero_rows, sem) = refs[:-2], refs[-2:]
    tile = weights.shape[2]
    slots = weights.shape[1]
    filled = [
        (outs[at].at[i] if len(outs[at].shape) == 3 else outs[at], s, first)
        for at, i, s, first in pieces
    ]
    zero_rows[...] = jnp.zeros_like(zero_rows)

    def clear(ref, i):
        return pltpu.make_async_copy(zero_rows, ref.at[pl.ds(i * tile, tile), :], sem)

    for ref, _, _ in filled:

        @pl.loop(0, ref.shape[0] // tile)
        def _(i, ref=ref):
            clear(ref, i).start()

    for ref, _, _ in filled:

        @pl.loop(0, ref.shape[0] // tile)
        def _(i, ref=ref):
            clear(ref, i).wait()

    started = jnp.int32(0)
    for ref, s, first in filled:
        held = ref.shape[0] // tile
        whole = held * tile == zero_rows.shape[1]

        def place_slot(k, total, ref=ref, s=s, first=first, held=held, whole=whole):
            spot = table[s, k]
            row, col = (spot >> SHIFT) - first, spot & ((1 << SHIFT) - 1)

            def start():
                pltpu.make_async_copy(
                    weights.at[s, k],
                    ref.at[
                        pl.ds(pl.multiple_of(row * tile, tile), tile),
                        pl.ds(pl.multiple_of(col * tile, tile), tile),
                    ],
                    sem,
                ).start()

            if whole:
                start()
                return total + 1
            inside = jnp.logical_and(row >= 0, row < held)
            pl.when(inside)(start)
            return total + inside.astype(jnp.int32)

        started = lax.fori_loop(0, table[s, slots], place_slot, started)

    largest = 1
    while largest * 2 <= slots:
        largest *= 2

    def wait(tiles):
        some = weights.at[0, pl.ds(0, tiles)]
        pltpu.make_async_copy(some, some, sem).wait()

    @pl.loop(0, started // largest)
    def _(_):
        wait(largest)

    amount = largest // 2
    while amount:

        @pl.when(started & amount != 0)
        def _(amount=amount):
            wait(amount)

        amount //= 2


def densify(limit, table, weights, pieces, out_shape, name):
    tile = weights.shape[2]
    nodes = out_shape[0].shape[-1]
    hbm = pl.BlockSpec(memory_space=pl.ANY)
    size = sum(v.size for v in out_shape)
    return pl.pallas_call(
        functools.partial(densify_kernel, pieces),
        out_shape=out_shape,
        in_specs=[pl.BlockSpec(memory_space=pltpu.SMEM), hbm],
        out_specs=(hbm,) * len(out_shape),
        scratch_shapes=[pltpu.VMEM((tile, nodes), BF16), pltpu.SemaphoreType.DMA],
        compiler_params=pltpu.CompilerParams(vmem_limit_bytes=limit),
        cost_estimate=pl.CostEstimate(flops=0, bytes_accessed=6 * size, transcendentals=0),
        name=name,
    )(table, weights)


def spot_table(rows, cols, counts, order, part_tiles):
    part = rows // part_tiles
    row = rows % part_tiles
    for g, at in enumerate(order):
        row = row + jnp.where(part == g, at * part_tiles, 0)
    return jnp.concatenate([(row << SHIFT) + cols, counts[:, None]], axis=1)


def either(at, blocks, run):
    if len(blocks) == 1:
        run(blocks[0])
        return
    for i, block in enumerate(blocks):
        pl.when(at == i)(functools.partial(run, block))


def pick_early():
    rep, _, _ = position()
    return jnp.where(rep == 0, 0, jnp.where(rep == lax.axis_size("rep") // 2, 1, 2))


def pick_late():
    rep, _, _ = position()
    odd = lax.axis_index("dom").astype(jnp.int32) % 2
    return jnp.where(rep == 1 - odd, 2, jnp.where(rep == lax.axis_size("rep") // 2 + 1 - odd, 1, 0))


def early_kernel(dense, *refs):
    found, outs = refs[:-4], refs[-4:]

    def run(*blocks):
        at = 0
        for out in outs:
            rows = slice(at, at + out.shape[0])
            total = jnp.dot(dense[0, rows, :], blocks[0][...], preferred_element_type=F32)
            for s in range(1, len(blocks)):
                total = total + jnp.dot(dense[s, rows, :], blocks[s][...], preferred_element_type=F32)
            out[...] = total
            at += out.shape[0]

    if dense.shape[0] > 1:
        run(*found)
    else:
        either(pick_early(), found, run)


def rows_kernel(begun, dense, *refs):
    found, out = refs[:-1], refs[-1]

    def run(block):
        out[...] = begun[...] + jnp.dot(dense[...], block[...], preferred_element_type=F32)

    either(pick_late(), found, run)


def mid_kernel(received, begun, dense, *refs):
    found, out = refs[:-1], refs[-1]

    def run(block):
        total = begun[...] + jnp.dot(dense[...], block[...], preferred_element_type=F32)
        out[...] = (total + received[...]).astype(out.dtype)

    either(pick_late(), found, run)


def own_kernel(features, received, weight_self, begun, dense, *refs):
    found, (own, projected) = refs[:-2], refs[-2:]
    part = own.shape[0]
    rep, _, _ = position()

    def run(block):
        total = begun[...] + jnp.dot(dense[...], block[...], preferred_element_type=F32)
        own[...] = total + received[...]

    either(pick_late(), found, run)
    mine = features[pl.ds(pl.multiple_of(rep * part, part), part), :]
    projected[...] = jnp.dot(mine, weight_self[...], preferred_element_type=F32)


def vmem_call(limit, kernel, out_shape, operands, name, flops=0):
    vmem = pl.BlockSpec(memory_space=pltpu.VMEM)
    held = sum(v.size * v.dtype.itemsize for v in (*operands, *jax.tree.leaves(out_shape)))
    return pl.pallas_call(
        kernel,
        out_shape=out_shape,
        in_specs=[vmem] * len(operands),
        out_specs=jax.tree.map(lambda _: vmem, out_shape),
        compiler_params=pltpu.CompilerParams(vmem_limit_bytes=limit),
        cost_estimate=pl.CostEstimate(flops=flops, bytes_accessed=held, transcendentals=0),
        name=name,
    )(*operands)


def layer_kernel(
    features, own, side, projected, weight_neigh, cotangent, out, grad_keep, grad_send
):
    part = own.shape[0]
    rep, _, core = position()
    mine = features[pl.ds(pl.multiple_of(rep * part, part), part), :]
    aggregate = (own[...] + side[...].astype(F32)).astype(BF16)
    pre = projected[...] + jnp.dot(aggregate, weight_neigh[...], preferred_element_type=F32)
    sigmoid = jax.nn.sigmoid(pre)
    out[...] = (pre * sigmoid).astype(BF16)
    slope = (cotangent[...].astype(F32) * sigmoid * (1.0 + pre * (1.0 - sigmoid))).astype(BF16)
    contract = (((0,), (0,)), ((), ()))
    grad_self = lax.dot_general(mine, slope, contract, preferred_element_type=F32)
    grad_neigh = lax.dot_general(aggregate, slope, contract, preferred_element_type=F32)
    first = core == 0
    grad_keep[...] = jnp.where(first, grad_self, grad_neigh)
    grad_send[...] = jnp.where(first, grad_neigh, grad_self)


def all_reduce_grads(core, keep, send, devices, groups):
    rows, width = keep.shape
    chunk = rows // devices
    chip = (keep + rep_exchange(send, groups, 0)).astype(BF16)
    terms = lax.all_to_all(chip, AXES, 0, 0, tiled=True)
    summed = terms.reshape(devices // 2, 2, chunk, width).astype(F32).sum(0).astype(BF16)
    spread = jnp.broadcast_to(summed[None], (devices // 2, 2, chunk, width)).reshape(rows, width)
    mine = lax.all_to_all(spread, AXES, 0, 0, tiled=True)
    other = rep_exchange(mine, groups, 0)
    first = core == 0
    grad_self = jnp.where(first, mine, other).astype(F32)
    grad_neigh = jnp.where(first, other, mine).astype(F32)
    return grad_self, grad_neigh


def on_device(
    features, tile_weights, tile_rows, tile_cols, tile_counts, weight_self, weight_neigh, cotangent
):
    blocks, groups = lax.axis_size("dom"), lax.axis_size("rep")
    steps = tile_weights.shape[2]
    nodes, width = features.shape
    rep, side_at, core = position()
    half = groups // 2
    order = [
        jnp.where(core == g % 2, half, 0) + jnp.where(side_at == g // 2, 1, 0) for g in range(groups)
    ]
    part = nodes // groups
    part_tiles = part // tile_weights.shape[-1]
    table = spot_table(tile_rows[0, 0], tile_cols[0, 0], tile_counts[0, 0], order, part_tiles)
    weights = tile_weights[0, 0]
    limit = 2 * ((steps - 1) * nodes + (steps + 1) * width) * nodes + 4 * nodes * width + 8 * MIB
    row_parts = jax.ShapeDtypeStruct((part, nodes), BF16)
    later = jax.ShapeDtypeStruct((steps - 1, nodes, nodes), BF16)
    send_pieces = ((0, 0, 0, 0), (1, 0, 0, part_tiles))
    rest_pieces = tuple((0, s - 1, s, 0) for s in range(1, steps)) + (
        (1, 0, 0, half * part_tiles),
        (2, 0, 0, (half + 1) * part_tiles),
    )

    special = steps == 2 and groups == 4 and blocks == steps * groups
    routes = Routes(blocks, groups)
    move = lambda value, source: flat_permute(value, blocks, groups, source)
    waited = features
    if special:
        ahead = move(features, routes.ahead)
    dense_send = densify(limit, table, weights, send_pieces, (row_parts,) * half, "densify_send")
    if special:
        waited, dense_send = lax.optimization_barrier((features, dense_send))
        early_found = (features, ahead, move(waited, routes.later))
        late_found = (move(waited, routes.first), move(ahead, routes.passed), ahead)
    else:
        late, *early_found = fetch_blocks(features, blocks, groups, steps)
        late_found = (late,)
    early, dense_mid, dense_own = densify(
        limit, table, weights, rest_pieces, (later, row_parts, row_parts), "densify_rest"
    )
    quarter = jax.ShapeDtypeStruct((part, width), F32)
    square = jax.ShapeDtypeStruct((width, width), F32)
    per_row = 2 * nodes * width
    *begun_send, begun_mid, begun_own = vmem_call(
        limit,
        early_kernel,
        (quarter,) * groups,
        (early, *early_found),
        "early_rows",
        (steps - 1) * nodes * per_row,
    )
    send = [
        vmem_call(limit, rows_kernel, quarter, (begun, dense, *late_found), name, part * per_row)
        for begun, dense, name in zip(begun_send, dense_send, ("send_other_side", "send_this_side"))
    ]
    received = [rep_exchange(rows, groups, 0) for rows in send]
    across = vmem_call(
        limit,
        mid_kernel,
        jax.ShapeDtypeStruct((part, width), BF16),
        (received[0], begun_mid, dense_mid, *late_found),
        "mid_rows",
        part * per_row,
    )
    side = rep_exchange(across, groups, 1)
    own, projected = vmem_call(
        limit,
        own_kernel,
        (quarter, quarter),
        (features, received[1], weight_self, begun_own, dense_own, *late_found),
        "own_rows",
        part * per_row,
    )
    out, grad_keep, grad_send = vmem_call(
        limit,
        layer_kernel,
        (jax.ShapeDtypeStruct((part, width), BF16), square, square),
        (features, own, side, projected, weight_neigh, cotangent),
        "layer",
        6 * part * width * width,
    )
    grad_self, grad_neigh = all_reduce_grads(core, grad_keep, grad_send, blocks * groups, groups)
    return out, grad_self, grad_neigh


def solution(mesh):
    return jax.shard_map(
        on_device,
        mesh=mesh,
        in_specs=(
            P("dom", None),
            P("dom", "rep", None, None, None, None),
            P("dom", "rep", None, None),
            P("dom", "rep", None, None),
            P("dom", "rep", None),
            P(),
            P(),
            P(AXES, None),
        ),
        out_specs=(P(AXES, None), P(), P()),
        check_vma=False,
    )
```

```python
import functools

import jax
import jax.numpy as jnp
from jax import lax
from jax.experimental import pallas as pl
from jax.experimental.pallas import tpu as pltpu
from jax.sharding import PartitionSpec as P

AXES = ("dom", "rep")
F32, BF16 = jnp.float32, jnp.bfloat16
MIB = 1 << 20
SHIFT = 16


def position():
    rep = lax.axis_index("rep").astype(jnp.int32)
    return rep, rep // 2, rep % 2


def flat_permute(value, blocks, groups, source):
    route = []
    for p in range(blocks):
        for r in range(groups):
            at = source(p, r)
            if at is not None:
                route.append((at[0] % blocks * groups + at[1] % groups, p * groups + r))
    return lax.ppermute(value, AXES, route)


def rep_exchange(value, groups, bit):
    route = [(r, r ^ (1 << bit)) for r in range(groups)]
    return lax.ppermute(value, "rep", route)


def fetch_blocks(features, blocks, groups, steps):
    found = []
    for s in range(steps):
        flip = groups // 2 if s % 2 else 0

        def source(p, r, s=s, flip=flip):
            return p + r * steps + s - steps // 2, r ^ flip

        found.append(flat_permute(features, blocks, groups, source))
    return found


class Routes:
    def __init__(self, blocks, groups):
        self.blocks, self.half, self.last = blocks, groups // 2, groups - 1

    def ahead(self, p, r):
        if r == self.half:
            q = (p + 2 * r) % self.blocks
            return q, self.half if q // 2 % 2 else 0
        return (p + 2 * r - 1, 1) if r == 1 - p % 2 else None

    def passed(self, p, r):
        if p % 2 and r == self.half:
            return p - 1, r
        if p % 2 == 0 and r == self.last:
            return p + 1, r - 1
        return None

    def second(self, p, r):
        if r == 1:
            return p + 2 * r, self.last
        return (p + 2 * r - 1, 1) if r == self.last and p % 2 else None

    def third(self, p, r):
        if r == self.last:
            return p + 2 * r, self.last
        if p % 2:
            return (p + 2 * r - 1, 1) if r == 1 else None
        return None if r == 1 else (p + 2 * r - 1, 0 if r else 1)


def densify_kernel(pieces, table, weights, *refs):
    outs, (zero_rows, sem) = refs[:-2], refs[-2:]
    tile = weights.shape[2]
    slots = weights.shape[1]
    filled = [
        (outs[at].at[i] if len(outs[at].shape) == 3 else outs[at], s, first)
        for at, i, s, first in pieces
    ]
    zero_rows[...] = jnp.zeros_like(zero_rows)

    def clear(ref, i):
        return pltpu.make_async_copy(zero_rows, ref.at[pl.ds(i * tile, tile), :], sem)

    for ref, _, _ in filled:

        @pl.loop(0, ref.shape[0] // tile)
        def _(i, ref=ref):
            clear(ref, i).start()

    for ref, _, _ in filled:

        @pl.loop(0, ref.shape[0] // tile)
        def _(i, ref=ref):
            clear(ref, i).wait()

    started = jnp.int32(0)
    for ref, s, first in filled:
        held = ref.shape[0] // tile
        whole = held * tile == zero_rows.shape[1]

        def place_slot(k, total, ref=ref, s=s, first=first, held=held, whole=whole):
            spot = table[s, k]
            row, col = (spot >> SHIFT) - first, spot & ((1 << SHIFT) - 1)

            def start():
                pltpu.make_async_copy(
                    weights.at[s, k],
                    ref.at[
                        pl.ds(pl.multiple_of(row * tile, tile), tile),
                        pl.ds(pl.multiple_of(col * tile, tile), tile),
                    ],
                    sem,
                ).start()

            if whole:
                start()
                return total + 1
            inside = jnp.logical_and(row >= 0, row < held)
            pl.when(inside)(start)
            return total + inside.astype(jnp.int32)

        started = lax.fori_loop(0, table[s, slots], place_slot, started)

    largest = 1
    while largest * 2 <= slots:
        largest *= 2

    def wait(tiles):
        some = weights.at[0, pl.ds(0, tiles)]
        pltpu.make_async_copy(some, some, sem).wait()

    @pl.loop(0, started // largest)
    def _(_):
        wait(largest)

    amount = largest // 2
    while amount:

        @pl.when(started & amount != 0)
        def _(amount=amount):
            wait(amount)

        amount //= 2


def densify(limit, table, weights, pieces, out_shape, name):
    tile = weights.shape[2]
    nodes = out_shape[0].shape[-1]
    hbm = pl.BlockSpec(memory_space=pl.ANY)
    size = sum(v.size for v in out_shape)
    return pl.pallas_call(
        functools.partial(densify_kernel, pieces),
        out_shape=out_shape,
        in_specs=[pl.BlockSpec(memory_space=pltpu.SMEM), hbm],
        out_specs=(hbm,) * len(out_shape),
        scratch_shapes=[pltpu.VMEM((tile, nodes), BF16), pltpu.SemaphoreType.DMA],
        compiler_params=pltpu.CompilerParams(vmem_limit_bytes=limit),
        cost_estimate=pl.CostEstimate(flops=0, bytes_accessed=6 * size, transcendentals=0),
        name=name,
    )(table, weights)


def spot_table(rows, cols, counts, order, part_tiles):
    part = rows // part_tiles
    row = rows % part_tiles
    for g, at in enumerate(order):
        row = row + jnp.where(part == g, at * part_tiles, 0)
    return jnp.concatenate([(row << SHIFT) + cols, counts[:, None]], axis=1)


def either(at, blocks, run):
    if len(blocks) == 1:
        run(blocks[0])
        return
    for i, block in enumerate(blocks):
        pl.when(at == i)(functools.partial(run, block))


def pick_early():
    rep, _, _ = position()
    half = lax.axis_size("rep") // 2
    return jnp.where(rep == 0, 0, jnp.where(rep == half, 1, jnp.where(rep == 1, 2, 3)))


def pick_late():
    rep, _, _ = position()
    odd = lax.axis_index("dom").astype(jnp.int32) % 2
    half = lax.axis_size("rep") // 2
    others = jnp.where(jnp.logical_and(rep == half + 1, odd == 1), 2, 3)
    return jnp.where(rep == 1 - odd, 0, jnp.where(rep == half + 1 - odd, 1, others))


def early_kernel(dense, *refs):
    found, outs = refs[:-4], refs[-4:]

    def run(*blocks):
        at = 0
        for out in outs:
            rows = slice(at, at + out.shape[0])
            total = jnp.dot(dense[0, rows, :], blocks[0][...], preferred_element_type=F32)
            for s in range(1, len(blocks)):
                total = total + jnp.dot(dense[s, rows, :], blocks[s][...], preferred_element_type=F32)
            out[...] = total
            at += out.shape[0]

    if dense.shape[0] > 1:
        run(*found)
    else:
        either(pick_early(), found, run)


def rows_kernel(begun, dense, *refs):
    found, out = refs[:-1], refs[-1]

    def run(block):
        out[...] = begun[...] + jnp.dot(dense[...], block[...], preferred_element_type=F32)

    either(pick_late(), found, run)


def mid_kernel(received, begun, dense, *refs):
    found, out = refs[:-1], refs[-1]

    def run(block):
        total = begun[...] + jnp.dot(dense[...], block[...], preferred_element_type=F32)
        out[...] = (total + received[...]).astype(out.dtype)

    either(pick_late(), found, run)


def own_kernel(features, received, weight_self, begun, dense, *refs):
    found, (own, projected) = refs[:-2], refs[-2:]
    part = own.shape[0]
    rep, _, _ = position()

    def run(block):
        total = begun[...] + jnp.dot(dense[...], block[...], preferred_element_type=F32)
        own[...] = total + received[...]

    either(pick_late(), found, run)
    mine = features[pl.ds(pl.multiple_of(rep * part, part), part), :]
    projected[...] = jnp.dot(mine, weight_self[...], preferred_element_type=F32)


def vmem_call(limit, kernel, out_shape, operands, name, flops=0):
    vmem = pl.BlockSpec(memory_space=pltpu.VMEM)
    held = sum(v.size * v.dtype.itemsize for v in (*operands, *jax.tree.leaves(out_shape)))
    return pl.pallas_call(
        kernel,
        out_shape=out_shape,
        in_specs=[vmem] * len(operands),
        out_specs=jax.tree.map(lambda _: vmem, out_shape),
        compiler_params=pltpu.CompilerParams(vmem_limit_bytes=limit),
        cost_estimate=pl.CostEstimate(flops=flops, bytes_accessed=held, transcendentals=0),
        name=name,
    )(*operands)


def layer_kernel(
    features, own, side, projected, weight_neigh, cotangent, out, grad_keep, grad_send
):
    part = own.shape[0]
    rep, _, core = position()
    mine = features[pl.ds(pl.multiple_of(rep * part, part), part), :]
    aggregate = (own[...] + side[...].astype(F32)).astype(BF16)
    pre = projected[...] + jnp.dot(aggregate, weight_neigh[...], preferred_element_type=F32)
    sigmoid = jax.nn.sigmoid(pre)
    out[...] = (pre * sigmoid).astype(BF16)
    slope = (cotangent[...].astype(F32) * sigmoid * (1.0 + pre * (1.0 - sigmoid))).astype(BF16)
    contract = (((0,), (0,)), ((), ()))
    grad_self = lax.dot_general(mine, slope, contract, preferred_element_type=F32)
    grad_neigh = lax.dot_general(aggregate, slope, contract, preferred_element_type=F32)
    first = core == 0
    grad_keep[...] = jnp.where(first, grad_self, grad_neigh)
    grad_send[...] = jnp.where(first, grad_neigh, grad_self)


def all_reduce_grads(core, keep, send, devices, groups):
    rows, width = keep.shape
    chunk = rows // devices
    chip = (keep + rep_exchange(send, groups, 0)).astype(BF16)
    terms = lax.all_to_all(chip, AXES, 0, 0, tiled=True)
    summed = terms.reshape(devices // 2, 2, chunk, width).astype(F32).sum(0).astype(BF16)
    spread = jnp.broadcast_to(summed[None], (devices // 2, 2, chunk, width)).reshape(rows, width)
    mine = lax.all_to_all(spread, AXES, 0, 0, tiled=True)
    other = rep_exchange(mine, groups, 0)
    first = core == 0
    grad_self = jnp.where(first, mine, other).astype(F32)
    grad_neigh = jnp.where(first, other, mine).astype(F32)
    return grad_self, grad_neigh


def on_device(
    features, tile_weights, tile_rows, tile_cols, tile_counts, weight_self, weight_neigh, cotangent
):
    blocks, groups = lax.axis_size("dom"), lax.axis_size("rep")
    steps = tile_weights.shape[2]
    nodes, width = features.shape
    rep, side_at, core = position()
    half = groups // 2
    order = [
        jnp.where(core == g % 2, half, 0) + jnp.where(side_at == g // 2, 1, 0) for g in range(groups)
    ]
    part = nodes // groups
    part_tiles = part // tile_weights.shape[-1]
    table = spot_table(tile_rows[0, 0], tile_cols[0, 0], tile_counts[0, 0], order, part_tiles)
    weights = tile_weights[0, 0]
    limit = 2 * ((steps - 1) * nodes + (steps + 1) * width) * nodes + 4 * nodes * width + 8 * MIB
    row_parts = jax.ShapeDtypeStruct((part, nodes), BF16)
    later = jax.ShapeDtypeStruct((steps - 1, nodes, nodes), BF16)
    send_pieces = ((0, 0, 0, 0), (1, 0, 0, part_tiles))
    rest_pieces = tuple((0, s - 1, s, 0) for s in range(1, steps)) + (
        (1, 0, 0, half * part_tiles),
        (2, 0, 0, (half + 1) * part_tiles),
    )

    special = steps == 2 and groups == 4 and blocks == steps * groups
    routes = Routes(blocks, groups)
    move = lambda value, source: flat_permute(value, blocks, groups, source)
    waited = features
    if special:
        ahead = move(features, routes.ahead)
    dense_send = densify(limit, table, weights, send_pieces, (row_parts,) * half, "densify_send")
    if special:
        waited, dense_send = lax.optimization_barrier((features, dense_send))
        second, third = move(waited, routes.second), move(waited, routes.third)
        early_found = (features, ahead, second, third)
        late_found = (ahead, move(ahead, routes.passed), second, third)
    else:
        late, *early_found = fetch_blocks(features, blocks, groups, steps)
        late_found = (late,)
    early, dense_mid, dense_own = densify(
        limit, table, weights, rest_pieces, (later, row_parts, row_parts), "densify_rest"
    )
    quarter = jax.ShapeDtypeStruct((part, width), F32)
    square = jax.ShapeDtypeStruct((width, width), F32)
    per_row = 2 * nodes * width
    *begun_send, begun_mid, begun_own = vmem_call(
        limit,
        early_kernel,
        (quarter,) * groups,
        (early, *early_found),
        "early_rows",
        (steps - 1) * nodes * per_row,
    )
    send = [
        vmem_call(limit, rows_kernel, quarter, (begun, dense, *late_found), name, part * per_row)
        for begun, dense, name in zip(begun_send, dense_send, ("send_other_side", "send_this_side"))
    ]
    received = [rep_exchange(rows, groups, 0) for rows in send]
    across = vmem_call(
        limit,
        mid_kernel,
        jax.ShapeDtypeStruct((part, width), BF16),
        (received[0], begun_mid, dense_mid, *late_found),
        "mid_rows",
        part * per_row,
    )
    side = rep_exchange(across, groups, 1)
    own, projected = vmem_call(
        limit,
        own_kernel,
        (quarter, quarter),
        (features, received[1], weight_self, begun_own, dense_own, *late_found),
        "own_rows",
        part * per_row,
    )
    out, grad_keep, grad_send = vmem_call(
        limit,
        layer_kernel,
        (jax.ShapeDtypeStruct((part, width), BF16), square, square),
        (features, own, side, projected, weight_neigh, cotangent),
        "layer",
        6 * part * width * width,
    )
    grad_self, grad_neigh = all_reduce_grads(core, grad_keep, grad_send, blocks * groups, groups)
    return out, grad_self, grad_neigh


def solution(mesh):
    return jax.shard_map(
        on_device,
        mesh=mesh,
        in_specs=(
            P("dom", None),
            P("dom", "rep", None, None, None, None),
            P("dom", "rep", None, None),
            P("dom", "rep", None, None),
            P("dom", "rep", None),
            P(),
            P(),
            P(AXES, None),
        ),
        out_specs=(P(AXES, None), P(), P()),
        check_vma=False,
    )
```

```python
import functools

import jax
import jax.numpy as jnp
from jax import lax
from jax.experimental import pallas as pl
from jax.experimental.pallas import tpu as pltpu
from jax.sharding import PartitionSpec as P

AXES = ("dom", "rep")
F32, BF16 = jnp.float32, jnp.bfloat16
MIB = 1 << 20
SHIFT = 16


def position():
    rep = lax.axis_index("rep").astype(jnp.int32)
    return rep, rep // 2, rep % 2


def flat_permute(value, blocks, groups, source):
    route = []
    for p in range(blocks):
        for r in range(groups):
            at = source(p, r)
            if at is not None:
                route.append((at[0] % blocks * groups + at[1] % groups, p * groups + r))
    return lax.ppermute(value, AXES, route)


def rep_exchange(value, groups, bit):
    route = [(r, r ^ (1 << bit)) for r in range(groups)]
    return lax.ppermute(value, "rep", route)


def fetch_blocks(features, blocks, groups, steps):
    found = []
    for s in range(steps):
        flip = groups // 2 if s % 2 else 0

        def source(p, r, s=s, flip=flip):
            return p + r * steps + s - steps // 2, r ^ flip

        found.append(flat_permute(features, blocks, groups, source))
    return found


class Routes:
    def __init__(self, blocks, groups):
        self.blocks, self.half, self.last = blocks, groups // 2, groups - 1

    def ahead(self, p, r):
        if r == self.half:
            q = (p + 2 * r) % self.blocks
            return q, 0 if q // 2 % 2 else self.half
        return (p + 2 * r - 1, 1) if r == 1 - p % 2 else None

    def passed(self, p, r):
        if p % 2 and r == self.half:
            return p - 1, r
        if p % 2 == 0 and r == self.last:
            return p + 1, r - 1
        return None

    def second(self, p, r):
        if r == 1:
            return p + 2 * r, self.last
        return (p + 2 * r - 1, 0) if r == self.last and p % 2 else None

    def third(self, p, r):
        if r == self.last:
            return p + 2 * r, self.last
        if p % 2:
            return (p + 2 * r - 1, 1) if r == 1 else None
        return None if r == 1 else (p + 2 * r - 1, 1 if r else 0)


def densify_kernel(pieces, table, weights, *refs):
    outs, (zero_rows, sem) = refs[:-2], refs[-2:]
    tile = weights.shape[2]
    slots = weights.shape[1]
    filled = [
        (outs[at].at[i] if len(outs[at].shape) == 3 else outs[at], s, first)
        for at, i, s, first in pieces
    ]
    zero_rows[...] = jnp.zeros_like(zero_rows)

    def clear(ref, i):
        return pltpu.make_async_copy(zero_rows, ref.at[pl.ds(i * tile, tile), :], sem)

    for ref, _, _ in filled:

        @pl.loop(0, ref.shape[0] // tile)
        def _(i, ref=ref):
            clear(ref, i).start()

    for ref, _, _ in filled:

        @pl.loop(0, ref.shape[0] // tile)
        def _(i, ref=ref):
            clear(ref, i).wait()

    started = jnp.int32(0)
    for ref, s, first in filled:
        held = ref.shape[0] // tile
        whole = held * tile == zero_rows.shape[1]

        def place_slot(k, total, ref=ref, s=s, first=first, held=held, whole=whole):
            spot = table[s, k]
            row, col = (spot >> SHIFT) - first, spot & ((1 << SHIFT) - 1)

            def start():
                pltpu.make_async_copy(
                    weights.at[s, k],
                    ref.at[
                        pl.ds(pl.multiple_of(row * tile, tile), tile),
                        pl.ds(pl.multiple_of(col * tile, tile), tile),
                    ],
                    sem,
                ).start()

            if whole:
                start()
                return total + 1
            inside = jnp.logical_and(row >= 0, row < held)
            pl.when(inside)(start)
            return total + inside.astype(jnp.int32)

        started = lax.fori_loop(0, table[s, slots], place_slot, started)

    largest = 1
    while largest * 2 <= slots:
        largest *= 2

    def wait(tiles):
        some = weights.at[0, pl.ds(0, tiles)]
        pltpu.make_async_copy(some, some, sem).wait()

    @pl.loop(0, started // largest)
    def _(_):
        wait(largest)

    amount = largest // 2
    while amount:

        @pl.when(started & amount != 0)
        def _(amount=amount):
            wait(amount)

        amount //= 2


def densify(limit, table, weights, pieces, out_shape, name):
    tile = weights.shape[2]
    nodes = out_shape[0].shape[-1]
    hbm = pl.BlockSpec(memory_space=pl.ANY)
    size = sum(v.size for v in out_shape)
    return pl.pallas_call(
        functools.partial(densify_kernel, pieces),
        out_shape=out_shape,
        in_specs=[pl.BlockSpec(memory_space=pltpu.SMEM), hbm],
        out_specs=(hbm,) * len(out_shape),
        scratch_shapes=[pltpu.VMEM((tile, nodes), BF16), pltpu.SemaphoreType.DMA],
        compiler_params=pltpu.CompilerParams(vmem_limit_bytes=limit),
        cost_estimate=pl.CostEstimate(flops=0, bytes_accessed=6 * size, transcendentals=0),
        name=name,
    )(table, weights)


def spot_table(rows, cols, counts, order, part_tiles):
    part = rows // part_tiles
    row = rows % part_tiles
    for g, at in enumerate(order):
        row = row + jnp.where(part == g, at * part_tiles, 0)
    return jnp.concatenate([(row << SHIFT) + cols, counts[:, None]], axis=1)


def either(at, blocks, run):
    if len(blocks) == 1:
        run(blocks[0])
        return
    for i, block in enumerate(blocks):
        pl.when(at == i)(functools.partial(run, block))


def pick_early():
    rep, _, _ = position()
    half = lax.axis_size("rep") // 2
    return jnp.where(rep == 0, 0, jnp.where(rep == half, 1, jnp.where(rep == 1, 2, 3)))


def pick_late():
    rep, _, _ = position()
    odd = lax.axis_index("dom").astype(jnp.int32) % 2
    half = lax.axis_size("rep") // 2
    others = jnp.where(jnp.logical_and(rep == half + 1, odd == 1), 2, 3)
    return jnp.where(rep == 1 - odd, 0, jnp.where(rep == half + 1 - odd, 1, others))


def early_kernel(dense, *refs):
    found, outs = refs[:-4], refs[-4:]

    def run(*blocks):
        at = 0
        for out in outs:
            rows = slice(at, at + out.shape[0])
            total = jnp.dot(dense[0, rows, :], blocks[0][...], preferred_element_type=F32)
            for s in range(1, len(blocks)):
                total = total + jnp.dot(dense[s, rows, :], blocks[s][...], preferred_element_type=F32)
            out[...] = total
            at += out.shape[0]

    if dense.shape[0] > 1:
        run(*found)
    else:
        either(pick_early(), found, run)


def rows_kernel(begun, dense, *refs):
    found, out = refs[:-1], refs[-1]

    def run(block):
        out[...] = begun[...] + jnp.dot(dense[...], block[...], preferred_element_type=F32)

    either(pick_late(), found, run)


def mid_kernel(received, begun, dense, *refs):
    found, out = refs[:-1], refs[-1]

    def run(block):
        total = begun[...] + jnp.dot(dense[...], block[...], preferred_element_type=F32)
        out[...] = (total + received[...]).astype(out.dtype)

    either(pick_late(), found, run)


def own_kernel(features, received, weight_self, begun, dense, *refs):
    found, (own, projected) = refs[:-2], refs[-2:]
    part = own.shape[0]
    rep, _, _ = position()

    def run(block):
        total = begun[...] + jnp.dot(dense[...], block[...], preferred_element_type=F32)
        own[...] = total + received[...]

    either(pick_late(), found, run)
    mine = features[pl.ds(pl.multiple_of(rep * part, part), part), :]
    projected[...] = jnp.dot(mine, weight_self[...], preferred_element_type=F32)


def vmem_call(limit, kernel, out_shape, operands, name, flops=0):
    vmem = pl.BlockSpec(memory_space=pltpu.VMEM)
    held = sum(v.size * v.dtype.itemsize for v in (*operands, *jax.tree.leaves(out_shape)))
    return pl.pallas_call(
        kernel,
        out_shape=out_shape,
        in_specs=[vmem] * len(operands),
        out_specs=jax.tree.map(lambda _: vmem, out_shape),
        compiler_params=pltpu.CompilerParams(vmem_limit_bytes=limit),
        cost_estimate=pl.CostEstimate(flops=flops, bytes_accessed=held, transcendentals=0),
        name=name,
    )(*operands)


def layer_kernel(
    features, own, side, projected, weight_neigh, cotangent, out, grad_keep, grad_send
):
    part = own.shape[0]
    rep, _, core = position()
    mine = features[pl.ds(pl.multiple_of(rep * part, part), part), :]
    aggregate = (own[...] + side[...].astype(F32)).astype(BF16)
    pre = projected[...] + jnp.dot(aggregate, weight_neigh[...], preferred_element_type=F32)
    sigmoid = jax.nn.sigmoid(pre)
    out[...] = (pre * sigmoid).astype(BF16)
    slope = (cotangent[...].astype(F32) * sigmoid * (1.0 + pre * (1.0 - sigmoid))).astype(BF16)
    contract = (((0,), (0,)), ((), ()))
    grad_self = lax.dot_general(mine, slope, contract, preferred_element_type=F32)
    grad_neigh = lax.dot_general(aggregate, slope, contract, preferred_element_type=F32)
    first = core == 0
    grad_keep[...] = jnp.where(first, grad_self, grad_neigh)
    grad_send[...] = jnp.where(first, grad_neigh, grad_self)


def all_reduce_grads(core, keep, send, devices, groups):
    rows, width = keep.shape
    chunk = rows // devices
    chip = (keep + rep_exchange(send, groups, 0)).astype(BF16)
    terms = lax.all_to_all(chip, AXES, 0, 0, tiled=True)
    summed = terms.reshape(devices // 2, 2, chunk, width).astype(F32).sum(0).astype(BF16)
    spread = jnp.broadcast_to(summed[None], (devices // 2, 2, chunk, width)).reshape(rows, width)
    mine = lax.all_to_all(spread, AXES, 0, 0, tiled=True)
    other = rep_exchange(mine, groups, 0)
    first = core == 0
    grad_self = jnp.where(first, mine, other).astype(F32)
    grad_neigh = jnp.where(first, other, mine).astype(F32)
    return grad_self, grad_neigh


def on_device(
    features, tile_weights, tile_rows, tile_cols, tile_counts, weight_self, weight_neigh, cotangent
):
    blocks, groups = lax.axis_size("dom"), lax.axis_size("rep")
    steps = tile_weights.shape[2]
    nodes, width = features.shape
    rep, side_at, core = position()
    half = groups // 2
    order = [
        jnp.where(core == g % 2, half, 0) + jnp.where(side_at == g // 2, 1, 0) for g in range(groups)
    ]
    part = nodes // groups
    part_tiles = part // tile_weights.shape[-1]
    table = spot_table(tile_rows[0, 0], tile_cols[0, 0], tile_counts[0, 0], order, part_tiles)
    weights = tile_weights[0, 0]
    limit = 2 * ((steps - 1) * nodes + (steps + 1) * width) * nodes + 4 * nodes * width + 8 * MIB
    row_parts = jax.ShapeDtypeStruct((part, nodes), BF16)
    later = jax.ShapeDtypeStruct((steps - 1, nodes, nodes), BF16)
    send_pieces = ((0, 0, 0, 0), (1, 0, 0, part_tiles))
    rest_pieces = tuple((0, s - 1, s, 0) for s in range(1, steps)) + (
        (1, 0, 0, half * part_tiles),
        (2, 0, 0, (half + 1) * part_tiles),
    )

    special = steps == 2 and groups == 4 and blocks == steps * groups
    routes = Routes(blocks, groups)
    move = lambda value, source: flat_permute(value, blocks, groups, source)
    waited = features
    if special:
        ahead = move(features, routes.ahead)
    dense_send = densify(limit, table, weights, send_pieces, (row_parts,) * half, "densify_send")
    if special:
        waited, dense_send = lax.optimization_barrier((features, dense_send))
        second, third = move(waited, routes.second), move(waited, routes.third)
        early_found = (features, ahead, second, third)
        late_found = (ahead, move(ahead, routes.passed), second, third)
    else:
        late, *early_found = fetch_blocks(features, blocks, groups, steps)
        late_found = (late,)
    early, dense_mid, dense_own = densify(
        limit, table, weights, rest_pieces, (later, row_parts, row_parts), "densify_rest"
    )
    quarter = jax.ShapeDtypeStruct((part, width), F32)
    square = jax.ShapeDtypeStruct((width, width), F32)
    per_row = 2 * nodes * width
    *begun_send, begun_mid, begun_own = vmem_call(
        limit,
        early_kernel,
        (quarter,) * groups,
        (early, *early_found),
        "early_rows",
        (steps - 1) * nodes * per_row,
    )
    send = [
        vmem_call(limit, rows_kernel, quarter, (begun, dense, *late_found), name, part * per_row)
        for begun, dense, name in zip(begun_send, dense_send, ("send_other_side", "send_this_side"))
    ]
    received = [rep_exchange(rows, groups, 0) for rows in send]
    across = vmem_call(
        limit,
        mid_kernel,
        jax.ShapeDtypeStruct((part, width), BF16),
        (received[0], begun_mid, dense_mid, *late_found),
        "mid_rows",
        part * per_row,
    )
    side = rep_exchange(across, groups, 1)
    own, projected = vmem_call(
        limit,
        own_kernel,
        (quarter, quarter),
        (features, received[1], weight_self, begun_own, dense_own, *late_found),
        "own_rows",
        part * per_row,
    )
    out, grad_keep, grad_send = vmem_call(
        limit,
        layer_kernel,
        (jax.ShapeDtypeStruct((part, width), BF16), square, square),
        (features, own, side, projected, weight_neigh, cotangent),
        "layer",
        6 * part * width * width,
    )
    grad_self, grad_neigh = all_reduce_grads(core, grad_keep, grad_send, blocks * groups, groups)
    return out, grad_self, grad_neigh


def solution(mesh):
    return jax.shard_map(
        on_device,
        mesh=mesh,
        in_specs=(
            P("dom", None),
            P("dom", "rep", None, None, None, None),
            P("dom", "rep", None, None),
            P("dom", "rep", None, None),
            P("dom", "rep", None),
            P(),
            P(),
            P(AXES, None),
        ),
        out_specs=(P(AXES, None), P(), P()),
        check_vma=False,
    )
```

```python
import functools

import jax
import jax.numpy as jnp
from jax import lax
from jax.experimental import pallas as pl
from jax.experimental.pallas import tpu as pltpu
from jax.sharding import PartitionSpec as P

AXES = ("dom", "rep")
F32, BF16 = jnp.float32, jnp.bfloat16
MIB = 1 << 20
SHIFT = 16


def position():
    rep = lax.axis_index("rep").astype(jnp.int32)
    return rep, rep // 2, rep % 2


def flat_permute(value, blocks, groups, source):
    route = []
    for p in range(blocks):
        for r in range(groups):
            at = source(p, r)
            if at is not None:
                route.append((at[0] % blocks * groups + at[1] % groups, p * groups + r))
    return lax.ppermute(value, AXES, route)


def rep_exchange(value, groups, bit):
    route = [(r, r ^ (1 << bit)) for r in range(groups)]
    return lax.ppermute(value, "rep", route)


def fetch_blocks(features, blocks, groups, steps):
    found = []
    for s in range(steps):
        flip = groups // 2 if s % 2 else 0

        def source(p, r, s=s, flip=flip):
            return p + r * steps + s - steps // 2, r ^ flip

        found.append(flat_permute(features, blocks, groups, source))
    return found


class Routes:
    def __init__(self, blocks, groups):
        self.blocks, self.half, self.last = blocks, groups // 2, groups - 1

    def ahead(self, p, r):
        if r == self.half:
            q = (p + 2 * r) % self.blocks
            return q, 0 if q // 2 % 2 else self.half
        return (p + 2 * r - 1, 1) if r == 1 - p % 2 else None

    def passed(self, p, r):
        if p % 2 and r == self.half:
            return p - 1, r
        if p % 2 == 0 and r == self.last:
            return p + 1, r - 1
        return None

    def second(self, p, r):
        if r == 1:
            return p + 2 * r, self.last
        return (p + 2 * r - 1, 0) if r == self.last and p % 2 else None

    def third(self, p, r):
        if r == self.last:
            return p + 2 * r, self.last
        if p % 2:
            return (p + 2 * r - 1, 1) if r == 1 else None
        return None if r == 1 else (p + 2 * r - 1, 1 if r else 0)


def densify_kernel(pieces, table, weights, *refs):
    outs, (zero_rows, sem) = refs[:-2], refs[-2:]
    tile = weights.shape[2]
    slots = weights.shape[1]
    filled = [
        (outs[at].at[i] if len(outs[at].shape) == 3 else outs[at], s, first)
        for at, i, s, first in pieces
    ]
    zero_rows[...] = jnp.zeros_like(zero_rows)

    def clear(ref, i):
        return pltpu.make_async_copy(zero_rows, ref.at[pl.ds(i * tile, tile), :], sem)

    for ref, _, _ in filled:

        @pl.loop(0, ref.shape[0] // tile)
        def _(i, ref=ref):
            clear(ref, i).start()

    for ref, _, _ in filled:

        @pl.loop(0, ref.shape[0] // tile)
        def _(i, ref=ref):
            clear(ref, i).wait()

    started = jnp.int32(0)
    for ref, s, first in filled:
        held = ref.shape[0] // tile
        whole = held * tile == zero_rows.shape[1]

        def place_slot(k, total, ref=ref, s=s, first=first, held=held, whole=whole):
            spot = table[s, k]
            row, col = (spot >> SHIFT) - first, spot & ((1 << SHIFT) - 1)

            def start():
                pltpu.make_async_copy(
                    weights.at[s, k],
                    ref.at[
                        pl.ds(pl.multiple_of(row * tile, tile), tile),
                        pl.ds(pl.multiple_of(col * tile, tile), tile),
                    ],
                    sem,
                ).start()

            if whole:
                start()
                return total + 1
            inside = jnp.logical_and(row >= 0, row < held)
            pl.when(inside)(start)
            return total + inside.astype(jnp.int32)

        started = lax.fori_loop(0, table[s, slots], place_slot, started)

    largest = 1
    while largest * 2 <= slots:
        largest *= 2

    def wait(tiles):
        some = weights.at[0, pl.ds(0, tiles)]
        pltpu.make_async_copy(some, some, sem).wait()

    @pl.loop(0, started // largest)
    def _(_):
        wait(largest)

    amount = largest // 2
    while amount:

        @pl.when(started & amount != 0)
        def _(amount=amount):
            wait(amount)

        amount //= 2


def densify(limit, table, weights, pieces, out_shape, name):
    tile = weights.shape[2]
    nodes = out_shape[0].shape[-1]
    hbm = pl.BlockSpec(memory_space=pl.ANY)
    size = sum(v.size for v in out_shape)
    return pl.pallas_call(
        functools.partial(densify_kernel, pieces),
        out_shape=out_shape,
        in_specs=[pl.BlockSpec(memory_space=pltpu.SMEM), hbm],
        out_specs=(hbm,) * len(out_shape),
        scratch_shapes=[pltpu.VMEM((tile, nodes), BF16), pltpu.SemaphoreType.DMA],
        compiler_params=pltpu.CompilerParams(vmem_limit_bytes=limit),
        cost_estimate=pl.CostEstimate(flops=0, bytes_accessed=6 * size, transcendentals=0),
        name=name,
    )(table, weights)


def spot_table(rows, cols, counts, order, part_tiles):
    part = rows // part_tiles
    row = rows % part_tiles
    for g, at in enumerate(order):
        row = row + jnp.where(part == g, at * part_tiles, 0)
    return jnp.concatenate([(row << SHIFT) + cols, counts[:, None]], axis=1)


def either(at, blocks, run):
    if len(blocks) == 1:
        run(blocks[0])
        return
    for i, block in enumerate(blocks):
        pl.when(at == i)(functools.partial(run, block))


def pick_early():
    rep, _, _ = position()
    half = lax.axis_size("rep") // 2
    return jnp.where(rep == 0, 0, jnp.where(rep == half, 1, jnp.where(rep == 1, 2, 3)))


def pick_late():
    rep, _, _ = position()
    odd = lax.axis_index("dom").astype(jnp.int32) % 2
    half = lax.axis_size("rep") // 2
    others = jnp.where(jnp.logical_and(rep == half + 1, odd == 1), 2, 3)
    return jnp.where(rep == 1 - odd, 0, jnp.where(rep == half + 1 - odd, 1, others))


def early_kernel(dense, *refs):
    found, outs = refs[:-4], refs[-4:]

    def run(*blocks):
        at = 0
        for out in outs:
            rows = slice(at, at + out.shape[0])
            total = jnp.dot(dense[0, rows, :], blocks[0][...], preferred_element_type=F32)
            for s in range(1, len(blocks)):
                total = total + jnp.dot(dense[s, rows, :], blocks[s][...], preferred_element_type=F32)
            out[...] = total
            at += out.shape[0]

    if dense.shape[0] > 1:
        run(*found)
    else:
        either(pick_early(), found, run)


def rows_kernel(begun, dense, *refs):
    found, out = refs[:-1], refs[-1]

    def run(block):
        out[...] = begun[...] + jnp.dot(dense[...], block[...], preferred_element_type=F32)

    either(pick_late(), found, run)


def across_kernel(mid, received, out):
    out[...] = (mid[...] + received[...]).astype(out.dtype)


def own_kernel(features, received, weight_self, begun, dense, *refs):
    found, (own, projected) = refs[:-2], refs[-2:]
    part = own.shape[0]
    rep, _, _ = position()

    def run(block):
        total = begun[...] + jnp.dot(dense[...], block[...], preferred_element_type=F32)
        own[...] = total + received[...]

    either(pick_late(), found, run)
    mine = features[pl.ds(pl.multiple_of(rep * part, part), part), :]
    projected[...] = jnp.dot(mine, weight_self[...], preferred_element_type=F32)


def vmem_call(limit, kernel, out_shape, operands, name, flops=0):
    vmem = pl.BlockSpec(memory_space=pltpu.VMEM)
    held = sum(v.size * v.dtype.itemsize for v in (*operands, *jax.tree.leaves(out_shape)))
    return pl.pallas_call(
        kernel,
        out_shape=out_shape,
        in_specs=[vmem] * len(operands),
        out_specs=jax.tree.map(lambda _: vmem, out_shape),
        compiler_params=pltpu.CompilerParams(vmem_limit_bytes=limit),
        cost_estimate=pl.CostEstimate(flops=flops, bytes_accessed=held, transcendentals=0),
        name=name,
    )(*operands)


def layer_kernel(
    features, own, side, projected, weight_neigh, cotangent, out, grad_keep, grad_send
):
    part = own.shape[0]
    rep, _, core = position()
    mine = features[pl.ds(pl.multiple_of(rep * part, part), part), :]
    aggregate = (own[...] + side[...].astype(F32)).astype(BF16)
    pre = projected[...] + jnp.dot(aggregate, weight_neigh[...], preferred_element_type=F32)
    sigmoid = jax.nn.sigmoid(pre)
    out[...] = (pre * sigmoid).astype(BF16)
    slope = (cotangent[...].astype(F32) * sigmoid * (1.0 + pre * (1.0 - sigmoid))).astype(BF16)
    contract = (((0,), (0,)), ((), ()))
    grad_self = lax.dot_general(mine, slope, contract, preferred_element_type=F32)
    grad_neigh = lax.dot_general(aggregate, slope, contract, preferred_element_type=F32)
    first = core == 0
    grad_keep[...] = jnp.where(first, grad_self, grad_neigh)
    grad_send[...] = jnp.where(first, grad_neigh, grad_self)


def all_reduce_grads(core, keep, send, devices, groups):
    rows, width = keep.shape
    chunk = rows // devices
    chip = (keep + rep_exchange(send, groups, 0)).astype(BF16)
    terms = lax.all_to_all(chip, AXES, 0, 0, tiled=True)
    summed = terms.reshape(devices // 2, 2, chunk, width).astype(F32).sum(0).astype(BF16)
    spread = jnp.broadcast_to(summed[None], (devices // 2, 2, chunk, width)).reshape(rows, width)
    mine = lax.all_to_all(spread, AXES, 0, 0, tiled=True)
    other = rep_exchange(mine, groups, 0)
    first = core == 0
    grad_self = jnp.where(first, mine, other).astype(F32)
    grad_neigh = jnp.where(first, other, mine).astype(F32)
    return grad_self, grad_neigh


def on_device(
    features, tile_weights, tile_rows, tile_cols, tile_counts, weight_self, weight_neigh, cotangent
):
    blocks, groups = lax.axis_size("dom"), lax.axis_size("rep")
    steps = tile_weights.shape[2]
    nodes, width = features.shape
    rep, side_at, core = position()
    half = groups // 2
    order = [
        jnp.where(core == g % 2, half, 0) + jnp.where(side_at == g // 2, 1, 0) for g in range(groups)
    ]
    part = nodes // groups
    part_tiles = part // tile_weights.shape[-1]
    table = spot_table(tile_rows[0, 0], tile_cols[0, 0], tile_counts[0, 0], order, part_tiles)
    weights = tile_weights[0, 0]
    limit = 2 * ((steps - 1) * nodes + (steps + 1) * width) * nodes + 4 * nodes * width + 8 * MIB
    row_parts = jax.ShapeDtypeStruct((part, nodes), BF16)
    later = jax.ShapeDtypeStruct((steps - 1, nodes, nodes), BF16)
    send_pieces = ((0, 0, 0, 0), (1, 0, 0, part_tiles))
    rest_pieces = tuple((0, s - 1, s, 0) for s in range(1, steps)) + (
        (1, 0, 0, half * part_tiles),
        (2, 0, 0, (half + 1) * part_tiles),
    )

    special = steps == 2 and groups == 4 and blocks == steps * groups
    routes = Routes(blocks, groups)
    move = lambda value, source: flat_permute(value, blocks, groups, source)
    waited = features
    if special:
        ahead = move(features, routes.ahead)
    dense_send = densify(limit, table, weights, send_pieces, (row_parts,) * half, "densify_send")
    if special:
        waited, dense_send = lax.optimization_barrier((features, dense_send))
        second, third = move(waited, routes.second), move(waited, routes.third)
        early_found = (features, ahead, second, third)
        late_found = (ahead, move(ahead, routes.passed), second, third)
    else:
        late, *early_found = fetch_blocks(features, blocks, groups, steps)
        late_found = (late,)
    early, dense_mid, dense_own = densify(
        limit, table, weights, rest_pieces, (later, row_parts, row_parts), "densify_rest"
    )
    quarter = jax.ShapeDtypeStruct((part, width), F32)
    square = jax.ShapeDtypeStruct((width, width), F32)
    per_row = 2 * nodes * width
    *begun_send, begun_mid, begun_own = vmem_call(
        limit,
        early_kernel,
        (quarter,) * groups,
        (early, *early_found),
        "early_rows",
        (steps - 1) * nodes * per_row,
    )
    def late_rows(begun, dense, name):
        operands = (begun, dense, *late_found)
        return vmem_call(limit, rows_kernel, quarter, operands, name, part * per_row)

    other_side = rep_exchange(late_rows(begun_send[0], dense_send[0], "send_other_side"), groups, 0)
    mid = late_rows(begun_mid, dense_mid, "mid_rows")
    across_shape = jax.ShapeDtypeStruct((part, width), BF16)
    across = vmem_call(limit, across_kernel, across_shape, (mid, other_side), "across")
    side = rep_exchange(across, groups, 1)
    this_side = rep_exchange(late_rows(begun_send[1], dense_send[1], "send_this_side"), groups, 0)
    own, projected = vmem_call(
        limit,
        own_kernel,
        (quarter, quarter),
        (features, this_side, weight_self, begun_own, dense_own, *late_found),
        "own_rows",
        part * per_row,
    )
    out, grad_keep, grad_send = vmem_call(
        limit,
        layer_kernel,
        (jax.ShapeDtypeStruct((part, width), BF16), square, square),
        (features, own, side, projected, weight_neigh, cotangent),
        "layer",
        6 * part * width * width,
    )
    grad_self, grad_neigh = all_reduce_grads(core, grad_keep, grad_send, blocks * groups, groups)
    return out, grad_self, grad_neigh


def solution(mesh):
    return jax.shard_map(
        on_device,
        mesh=mesh,
        in_specs=(
            P("dom", None),
            P("dom", "rep", None, None, None, None),
            P("dom", "rep", None, None),
            P("dom", "rep", None, None),
            P("dom", "rep", None),
            P(),
            P(),
            P(AXES, None),
        ),
        out_specs=(P(AXES, None), P(), P()),
        check_vma=False,
    )
```

```python
import functools

import jax
import jax.numpy as jnp
from jax import lax
from jax.experimental import pallas as pl
from jax.experimental.pallas import tpu as pltpu
from jax.sharding import PartitionSpec as P

AXES = ("dom", "rep")
F32, BF16 = jnp.float32, jnp.bfloat16
MIB = 1 << 20
SHIFT = 16


def position():
    rep = lax.axis_index("rep").astype(jnp.int32)
    return rep, rep // 2, rep % 2


def flat_permute(value, blocks, groups, source):
    route = []
    for p in range(blocks):
        for r in range(groups):
            at = source(p, r)
            if at is not None:
                route.append((at[0] % blocks * groups + at[1] % groups, p * groups + r))
    return lax.ppermute(value, AXES, route)


def rep_exchange(value, groups, bit):
    route = [(r, r ^ (1 << bit)) for r in range(groups)]
    return lax.ppermute(value, "rep", route)


def fetch_blocks(features, blocks, groups, steps):
    found = []
    for s in range(steps):
        flip = groups // 2 if s % 2 else 0

        def source(p, r, s=s, flip=flip):
            return p + r * steps + s - steps // 2, r ^ flip

        found.append(flat_permute(features, blocks, groups, source))
    return found


class Routes:
    def __init__(self, blocks, groups):
        self.blocks, self.half, self.last = blocks, groups // 2, groups - 1

    def ahead(self, p, r):
        if r == self.half:
            q = (p + 2 * r) % self.blocks
            return q, 0 if q // 2 % 2 else self.half
        return (p + 2 * r - 1, 1) if r == 1 - p % 2 else None

    def passed(self, p, r):
        if p % 2 and r == self.half:
            return p - 1, r
        if p % 2 == 0 and r == self.last:
            return p + 1, r - 1
        return None

    def second(self, p, r):
        if r == 1:
            return p + 2 * r, self.last
        return (p + 2 * r - 1, 0) if r == self.last and p % 2 else None

    def third(self, p, r):
        if r == self.last:
            return p + 2 * r, self.last if p % 2 else 1
        if p % 2:
            return (p + 2 * r - 1, self.last) if r == 1 else None
        return None if r == 1 else (p + 2 * r - 1, 1 if r else 0)


def densify_kernel(pieces, table, weights, *refs):
    outs, (zero_rows, sem) = refs[:-2], refs[-2:]
    tile = weights.shape[2]
    slots = weights.shape[1]
    filled = [
        (outs[at].at[i] if len(outs[at].shape) == 3 else outs[at], s, first)
        for at, i, s, first in pieces
    ]
    zero_rows[...] = jnp.zeros_like(zero_rows)

    def clear(ref, i):
        return pltpu.make_async_copy(zero_rows, ref.at[pl.ds(i * tile, tile), :], sem)

    for ref, _, _ in filled:

        @pl.loop(0, ref.shape[0] // tile)
        def _(i, ref=ref):
            clear(ref, i).start()

    for ref, _, _ in filled:

        @pl.loop(0, ref.shape[0] // tile)
        def _(i, ref=ref):
            clear(ref, i).wait()

    started = jnp.int32(0)
    for ref, s, first in filled:
        held = ref.shape[0] // tile
        whole = held * tile == zero_rows.shape[1]

        def place_slot(k, total, ref=ref, s=s, first=first, held=held, whole=whole):
            spot = table[s, k]
            row, col = (spot >> SHIFT) - first, spot & ((1 << SHIFT) - 1)

            def start():
                pltpu.make_async_copy(
                    weights.at[s, k],
                    ref.at[
                        pl.ds(pl.multiple_of(row * tile, tile), tile),
                        pl.ds(pl.multiple_of(col * tile, tile), tile),
                    ],
                    sem,
                ).start()

            if whole:
                start()
                return total + 1
            inside = jnp.logical_and(row >= 0, row < held)
            pl.when(inside)(start)
            return total + inside.astype(jnp.int32)

        started = lax.fori_loop(0, table[s, slots], place_slot, started)

    largest = 1
    while largest * 2 <= slots:
        largest *= 2

    def wait(tiles):
        some = weights.at[0, pl.ds(0, tiles)]
        pltpu.make_async_copy(some, some, sem).wait()

    @pl.loop(0, started // largest)
    def _(_):
        wait(largest)

    amount = largest // 2
    while amount:

        @pl.when(started & amount != 0)
        def _(amount=amount):
            wait(amount)

        amount //= 2


def densify(limit, table, weights, pieces, out_shape, name):
    tile = weights.shape[2]
    nodes = out_shape[0].shape[-1]
    hbm = pl.BlockSpec(memory_space=pl.ANY)
    size = sum(v.size for v in out_shape)
    return pl.pallas_call(
        functools.partial(densify_kernel, pieces),
        out_shape=out_shape,
        in_specs=[pl.BlockSpec(memory_space=pltpu.SMEM), hbm],
        out_specs=(hbm,) * len(out_shape),
        scratch_shapes=[pltpu.VMEM((tile, nodes), BF16), pltpu.SemaphoreType.DMA],
        compiler_params=pltpu.CompilerParams(vmem_limit_bytes=limit),
        cost_estimate=pl.CostEstimate(flops=0, bytes_accessed=6 * size, transcendentals=0),
        name=name,
    )(table, weights)


def spot_table(rows, cols, counts, order, part_tiles):
    part = rows // part_tiles
    row = rows % part_tiles
    for g, at in enumerate(order):
        row = row + jnp.where(part == g, at * part_tiles, 0)
    return jnp.concatenate([(row << SHIFT) + cols, counts[:, None]], axis=1)


def either(at, blocks, run):
    if len(blocks) == 1:
        run(blocks[0])
        return
    for i, block in enumerate(blocks):
        pl.when(at == i)(functools.partial(run, block))


def pick_early():
    rep, _, _ = position()
    half = lax.axis_size("rep") // 2
    return jnp.where(rep == 0, 0, jnp.where(rep == half, 1, jnp.where(rep == 1, 2, 3)))


def pick_late():
    rep, _, _ = position()
    odd = lax.axis_index("dom").astype(jnp.int32) % 2
    half = lax.axis_size("rep") // 2
    others = jnp.where(jnp.logical_and(rep == half + 1, odd == 1), 2, 3)
    return jnp.where(rep == 1 - odd, 0, jnp.where(rep == half + 1 - odd, 1, others))


def early_kernel(dense, *refs):
    found, outs = refs[:-4], refs[-4:]

    def run(*blocks):
        at = 0
        for out in outs:
            rows = slice(at, at + out.shape[0])
            total = jnp.dot(dense[0, rows, :], blocks[0][...], preferred_element_type=F32)
            for s in range(1, len(blocks)):
                total = total + jnp.dot(dense[s, rows, :], blocks[s][...], preferred_element_type=F32)
            out[...] = total
            at += out.shape[0]

    if dense.shape[0] > 1:
        run(*found)
    else:
        either(pick_early(), found, run)


def rows_kernel(begun, dense, *refs):
    found, out = refs[:-1], refs[-1]

    def run(block):
        out[...] = begun[...] + jnp.dot(dense[...], block[...], preferred_element_type=F32)

    either(pick_late(), found, run)


def across_kernel(mid, received, out):
    out[...] = (mid[...] + received[...]).astype(out.dtype)


def own_kernel(features, received, weight_self, begun, dense, *refs):
    found, (own, projected) = refs[:-2], refs[-2:]
    part = own.shape[0]
    rep, _, _ = position()

    def run(block):
        total = begun[...] + jnp.dot(dense[...], block[...], preferred_element_type=F32)
        own[...] = total + received[...]

    either(pick_late(), found, run)
    mine = features[pl.ds(pl.multiple_of(rep * part, part), part), :]
    projected[...] = jnp.dot(mine, weight_self[...], preferred_element_type=F32)


def vmem_call(limit, kernel, out_shape, operands, name, flops=0):
    vmem = pl.BlockSpec(memory_space=pltpu.VMEM)
    held = sum(v.size * v.dtype.itemsize for v in (*operands, *jax.tree.leaves(out_shape)))
    return pl.pallas_call(
        kernel,
        out_shape=out_shape,
        in_specs=[vmem] * len(operands),
        out_specs=jax.tree.map(lambda _: vmem, out_shape),
        compiler_params=pltpu.CompilerParams(vmem_limit_bytes=limit),
        cost_estimate=pl.CostEstimate(flops=flops, bytes_accessed=held, transcendentals=0),
        name=name,
    )(*operands)


def layer_kernel(
    features, own, side, projected, weight_neigh, cotangent, out, grad_keep, grad_send
):
    part = own.shape[0]
    rep, _, core = position()
    mine = features[pl.ds(pl.multiple_of(rep * part, part), part), :]
    aggregate = (own[...] + side[...].astype(F32)).astype(BF16)
    pre = projected[...] + jnp.dot(aggregate, weight_neigh[...], preferred_element_type=F32)
    sigmoid = jax.nn.sigmoid(pre)
    out[...] = (pre * sigmoid).astype(BF16)
    slope = (cotangent[...].astype(F32) * sigmoid * (1.0 + pre * (1.0 - sigmoid))).astype(BF16)
    contract = (((0,), (0,)), ((), ()))
    grad_self = lax.dot_general(mine, slope, contract, preferred_element_type=F32)
    grad_neigh = lax.dot_general(aggregate, slope, contract, preferred_element_type=F32)
    first = core == 0
    grad_keep[...] = jnp.where(first, grad_self, grad_neigh)
    grad_send[...] = jnp.where(first, grad_neigh, grad_self)


def all_reduce_grads(core, keep, send, devices, groups):
    rows, width = keep.shape
    chunk = rows // devices
    chip = (keep + rep_exchange(send, groups, 0)).astype(BF16)
    terms = lax.all_to_all(chip, AXES, 0, 0, tiled=True)
    summed = terms.reshape(devices // 2, 2, chunk, width).astype(F32).sum(0).astype(BF16)
    spread = jnp.broadcast_to(summed[None], (devices // 2, 2, chunk, width)).reshape(rows, width)
    mine = lax.all_to_all(spread, AXES, 0, 0, tiled=True)
    other = rep_exchange(mine, groups, 0)
    first = core == 0
    grad_self = jnp.where(first, mine, other).astype(F32)
    grad_neigh = jnp.where(first, other, mine).astype(F32)
    return grad_self, grad_neigh


def on_device(
    features, tile_weights, tile_rows, tile_cols, tile_counts, weight_self, weight_neigh, cotangent
):
    blocks, groups = lax.axis_size("dom"), lax.axis_size("rep")
    steps = tile_weights.shape[2]
    nodes, width = features.shape
    rep, side_at, core = position()
    half = groups // 2
    order = [
        jnp.where(core == g % 2, half, 0) + jnp.where(side_at == g // 2, 1, 0) for g in range(groups)
    ]
    part = nodes // groups
    part_tiles = part // tile_weights.shape[-1]
    table = spot_table(tile_rows[0, 0], tile_cols[0, 0], tile_counts[0, 0], order, part_tiles)
    weights = tile_weights[0, 0]
    limit = 2 * ((steps - 1) * nodes + (steps + 1) * width) * nodes + 4 * nodes * width + 8 * MIB
    row_parts = jax.ShapeDtypeStruct((part, nodes), BF16)
    later = jax.ShapeDtypeStruct((steps - 1, nodes, nodes), BF16)
    send_pieces = ((0, 0, 0, 0), (1, 0, 0, part_tiles))
    rest_pieces = tuple((0, s - 1, s, 0) for s in range(1, steps)) + (
        (1, 0, 0, half * part_tiles),
        (2, 0, 0, (half + 1) * part_tiles),
    )

    special = steps == 2 and groups == 4 and blocks == steps * groups
    routes = Routes(blocks, groups)
    move = lambda value, source: flat_permute(value, blocks, groups, source)
    waited = features
    if special:
        ahead = move(features, routes.ahead)
    dense_send = densify(limit, table, weights, send_pieces, (row_parts,) * half, "densify_send")
    if special:
        waited, dense_send = lax.optimization_barrier((features, dense_send))
        second, third = move(waited, routes.second), move(waited, routes.third)
        early_found = (features, ahead, second, third)
        late_found = (ahead, move(ahead, routes.passed), second, third)
    else:
        late, *early_found = fetch_blocks(features, blocks, groups, steps)
        late_found = (late,)
    early, dense_mid, dense_own = densify(
        limit, table, weights, rest_pieces, (later, row_parts, row_parts), "densify_rest"
    )
    quarter = jax.ShapeDtypeStruct((part, width), F32)
    square = jax.ShapeDtypeStruct((width, width), F32)
    per_row = 2 * nodes * width
    *begun_send, begun_mid, begun_own = vmem_call(
        limit,
        early_kernel,
        (quarter,) * groups,
        (early, *early_found),
        "early_rows",
        (steps - 1) * nodes * per_row,
    )
    def late_rows(begun, dense, name):
        operands = (begun, dense, *late_found)
        return vmem_call(limit, rows_kernel, quarter, operands, name, part * per_row)

    other_side = rep_exchange(late_rows(begun_send[0], dense_send[0], "send_other_side"), groups, 0)
    mid = late_rows(begun_mid, dense_mid, "mid_rows")
    across_shape = jax.ShapeDtypeStruct((part, width), BF16)
    across = vmem_call(limit, across_kernel, across_shape, (mid, other_side), "across")
    side = rep_exchange(across, groups, 1)
    this_side = rep_exchange(late_rows(begun_send[1], dense_send[1], "send_this_side"), groups, 0)
    own, projected = vmem_call(
        limit,
        own_kernel,
        (quarter, quarter),
        (features, this_side, weight_self, begun_own, dense_own, *late_found),
        "own_rows",
        part * per_row,
    )
    out, grad_keep, grad_send = vmem_call(
        limit,
        layer_kernel,
        (jax.ShapeDtypeStruct((part, width), BF16), square, square),
        (features, own, side, projected, weight_neigh, cotangent),
        "layer",
        6 * part * width * width,
    )
    grad_self, grad_neigh = all_reduce_grads(core, grad_keep, grad_send, blocks * groups, groups)
    return out, grad_self, grad_neigh


def solution(mesh):
    return jax.shard_map(
        on_device,
        mesh=mesh,
        in_specs=(
            P("dom", None),
            P("dom", "rep", None, None, None, None),
            P("dom", "rep", None, None),
            P("dom", "rep", None, None),
            P("dom", "rep", None),
            P(),
            P(),
            P(AXES, None),
        ),
        out_specs=(P(AXES, None), P(), P()),
        check_vma=False,
    )
```
